32 devices in a mesh: mp: 4 (over y, x), dp: 8 (over z, core).
Axes of the slice: x: 2, y: 2, z: 4, core: 2. Of those that a mesh axis runs over, the one named last changes fastest.
Arguments:
- inputs: bfloat16 [1280, 8192], P('dp'), may hold values from -60 to 60
- cotangent: bfloat16 [1280, 16384], P('dp', 'mp'), may hold values from -11 to 11
- weight: float32 [8192, 16384], P('dp', 'mp'), may hold values from -6 to 6
- row_moment: float32 [8192], P('dp'), may hold values from 0.05 to 0.5
- col_moment: float32 [16384], P('mp'), may hold values from 0.01 to 60
Outputs:
- new_weight: float32 [8192, 16384], P('dp', 'mp')
- update: bfloat16 [8192, 16384], P('dp', 'mp')
- new_rows: float32 [8192], P('dp')
- new_cols: float32 [16384], P('mp')
The draws below stay inside these ranges and needn't reach their ends.
All inputs are finite; a program needn't handle non-finite values.
Results may differ from the reference program's by a relative error of at most 0.001.
Values may be sent and summed in bfloat16 or wider, within the bound.
A program may use at most 128 MiB of HBM per device.

```python
import math
import jax
import jax.numpy as jnp
from jax import lax

D = 8192
F = 16384
TOKENS = 1280


def scaled_field(key, rows, cols, factor):
    first, second, third = jax.random.split(key, 3)
    noise = jnp.clip(jax.random.normal(first, (rows, cols), jnp.float32), -4.0, 4.0)
    row_scale = jnp.exp(jax.random.uniform(second, (rows, 1), jnp.float32) * jnp.log(10.0)) / jnp.sqrt(10.0)
    ramp = 0.5 + jnp.arange(cols, dtype=jnp.float32) / cols
    col_scale = jnp.exp(jax.random.uniform(third, (1, cols), jnp.float32) * jnp.log(10.0)) / jnp.sqrt(10.0) * ramp
    return noise * row_scale * col_scale * factor


def draw_inputs(key, part):
    key = jax.random.fold_in(key, 11)
    return scaled_field(key, TOKENS, D, 1.0).astype(jnp.bfloat16)


def draw_cotangent(key, part):
    key = jax.random.fold_in(key, 23)
    factor = 0.7 / jnp.sqrt(jnp.float32(TOKENS))
    return scaled_field(key, TOKENS, F, factor).astype(jnp.bfloat16)


def draw_col_moment(key, part):
    key = jax.random.fold_in(key, 37)
    position = jnp.arange(F, dtype=jnp.float32) / F
    jitter = jnp.exp(jax.random.uniform(key, (F,), jnp.float32, -1.0, 1.0) * jnp.log(2.0))
    level = 1.3 - 2.6 * position
    return (jnp.exp(level * jnp.log(10.0)) * jitter).astype(jnp.float32)


def level_of(own_key, dims, shards, smallest, high):
    factor_of, own = 1.0, jax.random.fold_in(own_key, 6)
    for dim, blocks in shards:
        steps = jnp.exp(jax.random.uniform(jax.random.fold_in(own, dim), (blocks,), jnp.float32, smallest / len(shards), high / len(shards)))
        factor_of = factor_of * jnp.repeat(steps, dims[dim] // blocks).reshape([-1 if axis == dim else 1 for axis in range(len(dims))])
    return factor_of


def bell_draw(rng, shape, spread, reach, cuts=(), kind=jnp.bfloat16):
    array = jax.random.normal(rng, shape, jnp.float32) * spread
    if len(cuts) > 0:
        array = level_of(rng, shape, cuts, -0.22, 0.18) * array
    return jnp.clip(array, min=-reach, max=reach).astype(kind)


def setup_inputs(seed: int = 0) -> dict:
    key_of = jax.random.split(jax.random.key(seed), 6)
    inputs = draw_inputs(jax.random.fold_in(key_of[5], 71), 0)
    cotangent = draw_cotangent(jax.random.fold_in(key_of[5], 71), 0)
    weight = bell_draw(key_of[2], (D, F), 1.0, 6.0, ((0, 8), (1, 4)), jnp.float32)
    row_moment = jnp.clip(jnp.exp(math.log(0.5) - 2.3025851 * jax.random.uniform(key_of[3], (D,), jnp.float32) ** level_of(key_of[3], (D,), ((0, 8),), -0.2, 0.2)), 0.05, 0.5)
    col_moment = draw_col_moment(jax.random.fold_in(key_of[5], 71), 0)
    return {"inputs": inputs, "cotangent": cotangent, "weight": weight, "row_moment": row_moment, "col_moment": col_moment}


decay_rate = 1.0 - 10.0 ** (-0.8)
step_size = 0.05
tiny_eps = 1e-30

def reference(inputs, cotangent, weight, row_moment, col_moment):
    gradient = jnp.dot(inputs.T, cotangent, preferred_element_type=jnp.float32)
    squares = gradient * gradient + tiny_eps
    new_rows = decay_rate * row_moment + (1.0 - decay_rate) * (lax.optimization_barrier(jnp.sum(squares, axis=1)) / F)
    new_cols = decay_rate * col_moment + (1.0 - decay_rate) * (lax.optimization_barrier(jnp.sum(squares, axis=0)) / D)
    row_mean = jnp.sum(new_rows) / D
    scaled = gradient / jnp.sqrt(new_rows[:, None] * new_cols[None, :] / row_mean)
    update_rms = jnp.sqrt(jnp.sum(scaled * scaled) / (D * F))
    clipped = scaled / jnp.maximum(1.0, update_rms)
    weight_rms = jnp.sqrt(jnp.sum(weight * weight) / (D * F))
    new_weight = weight - step_size * weight_rms * clipped
    return (new_weight, clipped.astype(jnp.bfloat16), new_rows, new_cols)
```

```python
import functools

import jax
import jax.numpy as jnp
from jax import lax
from jax.experimental import pallas as pl
from jax.experimental.pallas import tpu as pltpu
from jax.sharding import PartitionSpec as P

decay_rate = 1.0 - 10.0 ** (-0.8)
step_size = 0.05
tiny_eps = 1e-30

LANES = 128
MESH = pl.DeviceIdType.MESH
F32 = jnp.float32


def gather_kernel(
    MP, DP, W, BM,
    x_ref, cot_ref, w_ref, rm_ref, cm_ref,
    g_ref, nr_ref, nc_ref, rs_ref, cs_ref, sc_ref,
    a_raw, a_t, call, wbuf, row_acc, inv_r, inv_c, row_slots, col_slots, s_slots, t_slots,
    own_sem, wsem, in_send, in_recv, fwd_send, up_send, dn_send, sib_send,
    lane_recv, sib_recv, row_send, row_recv, col_send, col_recv,
    s_send, s_recv, t_send, t_recv,
):
    m = lax.axis_index("mp")
    me = lax.axis_index("dp")
    z, c = me // 2, me % 2
    Z = DP // 2
    sib = me + 1 - 2 * c
    T = x_ref.shape[0]
    R, C = g_ref.shape
    NC = C // W
    G = W // LANES
    D, F = R * DP, C * MP

    barrier = pltpu.get_barrier_semaphore()

    def greet_dp(q, _):
        pl.semaphore_signal(barrier, inc=1, device_id={"dp": (me + q) % DP}, device_id_type=MESH)
        return 0

    def greet_mp(q, _):
        pl.semaphore_signal(barrier, inc=1, device_id={"mp": (m + q) % MP}, device_id_type=MESH)
        return 0

    lax.fori_loop(1, DP, greet_dp, 0)
    lax.fori_loop(1, MP, greet_mp, 0)
    pl.semaphore_wait(barrier, DP + MP - 2)

    def rows_of(s):
        return pl.ds(pl.multiple_of(s * T, T), T)

    def cols_of(j):
        return pl.ds(pl.multiple_of(j * W, W), W)

    def feat_cols(d):
        return pl.ds(pl.multiple_of(d * R, R), R)

    def remote(src, dst, send, recv, **to):
        return pltpu.make_async_remote_copy(
            src_ref=src, dst_ref=dst, send_sem=send, recv_sem=recv,
            device_id=to, device_id_type=MESH,
        )

    def taker(s, d):
        return (s + (MP // 2) * (d % 2)) % MP

    def push(d):
        return remote(x_ref.at[:, feat_cols(d)], a_raw.at[rows_of(me), :],
                      in_send.at[d], in_recv.at[me], dp=d)

    def spread(s, q):
        return remote(a_raw.at[rows_of(s), :], a_raw.at[rows_of(s), :],
                      fwd_send.at[s, q], in_recv.at[s], mp=(m + q) % MP)

    def cot_block(zs, lane, j):
        return call.at[rows_of(zs * 2 + lane), cols_of(j)]

    def up(zs, j, src=None):
        dst = cot_block(zs, c, j)
        return remote(dst if src is None else src, dst, up_send.at[zs, j], lane_recv.at[zs, j], dp=(me + 2) % DP)

    def down(zs, j, src=None):
        dst = cot_block(zs, c, j)
        return remote(dst if src is None else src, dst, dn_send.at[zs, j], lane_recv.at[zs, j], dp=(me + DP - 2) % DP)

    def across(zs, j, src=None):
        dst = cot_block(zs, c, j)
        return remote(dst if src is None else src, dst, sib_send.at[zs, j], sib_recv.at[zs, j], dp=sib)

    def across_in(zs, j):
        dst = cot_block(zs, 1 - c, j)
        return remote(dst, dst, sib_send.at[zs, j], sib_recv.at[zs, j], dp=sib)

    own_x = pltpu.make_async_copy(x_ref.at[:, feat_cols(me)], a_raw.at[rows_of(me), :], own_sem.at[0])
    own_c = pltpu.make_async_copy(cot_ref, call.at[rows_of(me), :], own_sem.at[1])

    def push_step(d, _):
        @pl.when(jnp.logical_and(d != me, taker(me, d) == m))
        def _():
            push(d).start()
        return 0

    lax.fori_loop(0, DP, push_step, 0)
    own_x.start()
    own_c.start()

    def first_send(j, _):
        src = cot_ref.at[:, cols_of(j)]

        @pl.when(z < Z - 1)
        def _():
            up(z, j, src).start()

        @pl.when(z > 0)
        def _():
            down(z, j, src).start()

        across(z, j, src).start()
        return 0

    lax.fori_loop(0, NC, first_send, 0)

    WB = wbuf.shape[1]
    NW = R // WB

    def wcopy(i, slot):
        return pltpu.make_async_copy(w_ref.at[pl.ds(pl.multiple_of(i * WB, WB), WB), :], wbuf.at[slot], wsem.at[slot])

    wcopy(0, 0).start()

    def wstep(i, acc):
        slot = lax.rem(i, 2)

        @pl.when(i + 1 < NW)
        def _():
            wcopy(i + 1, 1 - slot).start()

        wcopy(i, slot).wait()

        def wcol(j, acc):
            v = wbuf[slot, :, cols_of(j)]
            return acc + jnp.sum((v * v).reshape(WB // 8, 8, W), axis=0)

        return lax.fori_loop(0, NC, wcol, acc)

    wacc = lax.fori_loop(0, NW, wstep, jnp.zeros((8, W), F32))
    wsq = sum(wacc[:, q * LANES:(q + 1) * LANES] for q in range(G))
    s_slots[m, 1] = wsq

    def take_step(s, _):
        @pl.when(jnp.logical_and(s != me, taker(s, me) == m))
        def _():
            spread(s, 1).wait_recv()

            def hand(q, _):
                spread(s, q).start()
                return 0

            lax.fori_loop(1, MP, hand, 0)
        return 0

    lax.fori_loop(0, DP, take_step, 0)

    def relay(k, j):
        lo, hi = z - k, z + k

        @pl.when(lo >= 0)
        def _():
            up(lo, j).wait_recv()

            @pl.when(z < Z - 1)
            def _():
                up(lo, j).start()

            across(lo, j).start()

        @pl.when(hi < Z)
        def _():
            down(hi, j).wait_recv()

            @pl.when(z > 0)
            def _():
                down(hi, j).start()

            across(hi, j).start()

    def relay_step(i, _):
        relay(1 + i // NC, i % NC)
        return 0

    lax.fori_loop(0, (Z - 2) * NC, relay_step, 0)

    def rest_step(s, _):
        @pl.when(jnp.logical_and(s != me, taker(s, me) != m))
        def _():
            spread(s, 1).wait_recv()
        return 0

    lax.fori_loop(0, DP, rest_step, 0)
    own_x.wait()
    own_c.wait()

    def turn(i, _):
        cols = pl.ds(pl.multiple_of(i * LANES, LANES), LANES)
        a_t[cols, :] = a_raw[:, cols].T
        return 0

    lax.fori_loop(0, R // LANES, turn, 0)
    row_acc[...] = jnp.zeros_like(row_acc)

    def chunk(j, _):
        relay(Z - 1, j)

        def sib_wait(zs, _):
            across_in(zs, j).wait_recv()
            return 0

        lax.fori_loop(0, Z, sib_wait, 0)

        def tile(i, cacc):
            rows = pl.ds(pl.multiple_of(i * BM, BM), BM)
            gt = jnp.dot(a_t[rows, :], call[:, cols_of(j)], preferred_element_type=F32)
            g_ref[rows, cols_of(j)] = gt
            sq = gt * gt
            row_acc[rows, :] += sum(sq[:, q * LANES:(q + 1) * LANES] for q in range(G))
            return cacc + jnp.sum(sq.reshape(BM // 8, 8, W), axis=0)

        cacc = lax.fori_loop(0, R // BM, tile, jnp.zeros((8, W), F32))
        csum = jnp.sum(cacc, axis=0, keepdims=True)
        for q in range(G):
            col_slots[me, pl.ds(j * G + q, 1), :] = csum[:, q * LANES:(q + 1) * LANES]
        return 0

    lax.fori_loop(0, NC, chunk, 0)

    for i in range(R // LANES):
        block = row_acc[i * LANES:(i + 1) * LANES, :].T
        row_slots[m, i:i + 1, :] = jnp.sum(block, axis=0, keepdims=True)

    def share(slots, send, recv, axis, own, count):
        def at(q):
            return remote(slots.at[own], slots.at[own], send.at[q], recv.at[own], **{axis: (own + q) % count})

        def go(q, _):
            at(q).start()
            return 0

        lax.fori_loop(1, count, go, 0)

    def shared(slots, send, recv, axis, own, count):
        def done(q, _):
            src = (own + q) % count
            remote(slots.at[src], slots.at[src], send.at[q], recv.at[src], **{axis: src}).wait_recv()
            return 0

        lax.fori_loop(1, count, done, 0)

    def sent(slots, send, recv, axis, own, count):
        def done(q, _):
            remote(slots.at[own], slots.at[own], send.at[q], recv.at[own], **{axis: (own + q) % count}).wait_send()
            return 0

        lax.fori_loop(1, count, done, 0)

    rows_x = (row_slots, row_send, row_recv, "mp", m, MP)
    cols_x = (col_slots, col_send, col_recv, "dp", me, DP)
    s_x = (s_slots, s_send, s_recv, "mp", m, MP)
    t_x = (t_slots, t_send, t_recv, "dp", me, DP)

    def total(slots, count):
        return lax.fori_loop(1, count, lambda i, a: a + slots[i], slots[0])

    share(*cols_x)
    share(*rows_x)
    shared(*rows_x)
    new_rows = decay_rate * rm_ref[...] + (1.0 - decay_rate) * ((total(row_slots, MP) + F * tiny_eps) / F)
    nr_ref[...] = new_rows
    inv_rows = 1.0 / new_rows
    for i in range(R // LANES):
        inv_r[i * LANES:(i + 1) * LANES, :] = jnp.broadcast_to(inv_rows[i:i + 1, :], (LANES, LANES)).T
    shared(*cols_x)
    new_cols = decay_rate * cm_ref[...] + (1.0 - decay_rate) * ((total(col_slots, DP) + D * tiny_eps) / D)
    nc_ref[...] = new_cols
    inv_c[...] = 1.0 / new_cols
    cs_ref[...] = lax.rsqrt(new_cols)

    def s_tile(i, acc):
        rows = pl.ds(pl.multiple_of(i * LANES, LANES), LANES)

        def s_cols(j, part):
            for q in range(G):
                v = g_ref[rows, pl.ds(pl.multiple_of(j * W + q * LANES, LANES), LANES)]
                part = part + (v * v) * inv_c[pl.ds(j * G + q, 1), :]
            return part

        part = lax.fori_loop(0, NC, s_cols, jnp.zeros((LANES, LANES), F32))
        return acc + jnp.sum((part * inv_r[rows, :]).reshape(LANES // 8, 8, LANES), axis=0)

    s_slots[m, 0] = lax.fori_loop(0, R // LANES, s_tile, jnp.zeros((8, LANES), F32))
    share(*s_x)
    rs_ref[...] = lax.sqrt(inv_r[...])
    t_slots[me, 2] = jnp.broadcast_to(jnp.sum(new_rows, axis=0, keepdims=True), (8, LANES))
    shared(*s_x)
    t_slots[me, 0:2] = total(s_slots, MP)
    share(*t_x)
    shared(*t_x)
    sums = total(t_slots, DP)

    def whole(v):
        return jnp.sum(jnp.sum(v, axis=0, keepdims=True), axis=1, keepdims=True)

    row_mean = whole(sums[2, 0:1, :]) / D
    update_rms = jnp.sqrt(row_mean * whole(sums[0]) / (D * F))
    weight_rms = jnp.sqrt(whole(sums[1]) / (D * F))
    factor = jnp.sqrt(row_mean) / jnp.maximum(1.0, update_rms)
    sc_ref[0:8, :] = jnp.broadcast_to(factor, (8, LANES))
    sc_ref[8:16, :] = jnp.broadcast_to(step_size * weight_rms, (8, LANES))

    sent(*rows_x)
    sent(*cols_x)
    sent(*s_x)
    sent(*t_x)

    def push_done(d, _):
        @pl.when(jnp.logical_and(d != me, taker(me, d) == m))
        def _():
            push(d).wait_send()

        @pl.when(jnp.logical_and(d != me, taker(d, me) == m))
        def _():
            def hand(q, _):
                spread(d, q).wait_send()
                return 0

            lax.fori_loop(1, MP, hand, 0)
        return 0

    lax.fori_loop(0, DP, push_done, 0)

    def cot_done(i, _):
        zs, j = i // NC, i % NC

        @pl.when(jnp.logical_and(zs <= z, z < Z - 1))
        def _():
            up(zs, j).wait_send()

        @pl.when(jnp.logical_and(zs >= z, z > 0))
        def _():
            down(zs, j).wait_send()

        across(zs, j).wait_send()
        return 0

    lax.fori_loop(0, Z * NC, cot_done, 0)


def apply_kernel(BR, g_ref, w_ref, rs_ref, cs_ref, sc_ref, nw_ref, up_ref):
    R, C = g_ref.shape

    def body(g, w, rs, nw, u):
        f1 = sc_ref[0:1, :]
        f2 = sc_ref[8:9, :]
        rscale = rs[...] * f1
        for q in range(C // LANES):
            sl = slice(q * LANES, (q + 1) * LANES)
            clipped = g[:, sl] * (rscale * cs_ref[q:q + 1, :])
            nw[:, sl] = w[:, sl] - f2 * clipped
            u[:, sl] = clipped.astype(u.dtype)

    wide = pl.BlockSpec((BR, C), lambda i: (i, 0))
    pltpu.emit_pipeline(
        body,
        grid=(R // BR,),
        in_specs=[wide, wide, pl.BlockSpec((BR, LANES), lambda i: (i, 0))],
        out_specs=[wide, wide],
    )(g_ref, w_ref, rs_ref, nw_ref, up_ref)


def on_device(MP, DP, inputs, cotangent, weight, row_moment, col_moment):
    T = inputs.shape[0]
    R, C = weight.shape
    Z = DP // 2
    W = min(512, C)
    NC = C // W
    BM = min(512, R)
    WB = min(128, R)
    RT, CT = R // LANES, C // LANES
    vmem = pl.BlockSpec(memory_space=pltpu.VMEM)
    hbm = pl.BlockSpec(memory_space=pl.ANY)
    dma = pltpu.SemaphoreType.DMA
    g, nr, nc, rs, cs, sc = pl.pallas_call(
        functools.partial(gather_kernel, MP, DP, W, BM),
        out_shape=[
            pltpu.VMEM((R, C), F32),
            jax.ShapeDtypeStruct((RT, LANES), F32),
            jax.ShapeDtypeStruct((CT, LANES), F32),
            pltpu.VMEM((R, LANES), F32),
            pltpu.VMEM((CT, LANES), F32),
            pltpu.VMEM((16, LANES), F32),
        ],
        in_specs=[hbm, hbm, hbm, vmem, vmem],
        out_specs=[vmem] * 6,
        scratch_shapes=[
            pltpu.VMEM((T * DP, R), jnp.bfloat16),
            pltpu.VMEM((R, T * DP), jnp.bfloat16),
            pltpu.VMEM((T * DP, C), jnp.bfloat16),
            pltpu.VMEM((2, WB, C), F32),
            pltpu.VMEM((R, LANES), F32),
            pltpu.VMEM((R, LANES), F32),
            pltpu.VMEM((CT, LANES), F32),
            pltpu.VMEM((MP, RT, LANES), F32),
            pltpu.VMEM((DP, CT, LANES), F32),
            pltpu.VMEM((MP, 2, 8, LANES), F32),
            pltpu.VMEM((DP, 3, 8, LANES), F32),
            dma((2,)), dma((2,)), dma((DP,)), dma((DP,)), dma((DP, MP)),
            dma((Z, NC)), dma((Z, NC)), dma((Z, NC)), dma((Z, NC)), dma((Z, NC)),
            dma((MP,)), dma((MP,)), dma((DP,)), dma((DP,)),
            dma((MP,)), dma((MP,)), dma((DP,)), dma((DP,)),
        ],
        compiler_params=pltpu.CompilerParams(
            collective_id=0, has_side_effects=True, vmem_limit_bytes=44 * 2**20
        ),
        cost_estimate=pl.CostEstimate(flops=2 * R * C * T * DP, bytes_accessed=R * C * 4, transcendentals=0),
        name="gather_contract",
    )(inputs, cotangent, weight, row_moment.reshape(RT, LANES), col_moment.reshape(CT, LANES))
    BR = min(64, R)
    new_weight, update = pl.pallas_call(
        functools.partial(apply_kernel, BR),
        out_shape=[jax.ShapeDtypeStruct((R, C), F32), jax.ShapeDtypeStruct((R, C), jnp.bfloat16)],
        in_specs=[vmem, hbm, vmem, vmem, vmem],
        out_specs=[hbm, hbm],
        compiler_params=pltpu.CompilerParams(vmem_limit_bytes=32 * 2**20),
        cost_estimate=pl.CostEstimate(flops=4 * R * C, bytes_accessed=R * C * 10, transcendentals=0),
        name="apply_update",
    )(g, weight, rs, cs, sc)
    return new_weight, update, nr.reshape(R), nc.reshape(C)


def solution(mesh):
    return jax.shard_map(
        functools.partial(on_device, mesh.shape["mp"], mesh.shape["dp"]),
        mesh=mesh,
        in_specs=(P("dp", None), P("dp", "mp"), P("dp", "mp"), P("dp"), P("mp")),
        out_specs=(P("dp", "mp"), P("dp", "mp"), P("dp"), P("mp")),
        check_vma=False,
    )
```

```python
import functools

import jax
import jax.numpy as jnp
from jax import lax
from jax.experimental import pallas as pl
from jax.experimental.pallas import tpu as pltpu
from jax.sharding import PartitionSpec as P

decay_rate = 1.0 - 10.0 ** (-0.8)
step_size = 0.05
tiny_eps = 1e-30

LANES = 128
MESH = pl.DeviceIdType.MESH
F32 = jnp.float32


def gather_kernel(
    MP, DP, W, BM, LAG,
    x_ref, cot_ref, w_ref, rm_ref, cm_ref,
    buf,
    a_raw, a_t, call, row_acc, s_acc, inv_r, n_cols, row_slots, col_slots, s_slots, t_slots,
    own_sem, in_send, in_recv, fwd_send, up_send, dn_send, sib_send,
    lane_recv, sib_recv, row_send, row_recv, col_send, col_recv,
    s_send, s_recv, t_send, t_recv,
):
    m = lax.axis_index("mp")
    me = lax.axis_index("dp")
    z, c = me // 2, me % 2
    Z = DP // 2
    sib = me + 1 - 2 * c
    T = x_ref.shape[0]
    R, C = w_ref.shape
    RT, CT = R // LANES, C // LANES
    NC = C // W
    G = W // LANES
    D, F = R * DP, C * MP
    at_rows, at_cols, at_scale = extras(R, C)

    barrier = pltpu.get_barrier_semaphore()

    def greet_dp(q, _):
        pl.semaphore_signal(barrier, inc=1, device_id={"dp": (me + q) % DP}, device_id_type=MESH)
        return 0

    def greet_mp(q, _):
        pl.semaphore_signal(barrier, inc=1, device_id={"mp": (m + q) % MP}, device_id_type=MESH)
        return 0

    lax.fori_loop(1, DP, greet_dp, 0)
    lax.fori_loop(1, MP, greet_mp, 0)

    def rows_of(s):
        return pl.ds(pl.multiple_of(s * T, T), T)

    def cols_of(j):
        return pl.ds(pl.multiple_of(j * W, W), W)

    def feat_cols(d):
        return pl.ds(pl.multiple_of(d * R, R), R)

    own_x = pltpu.make_async_copy(x_ref.at[:, feat_cols(me)], a_raw.at[rows_of(me), :], own_sem.at[0])
    own_c = pltpu.make_async_copy(cot_ref, call.at[rows_of(me), :], own_sem.at[1])
    own_w = pltpu.make_async_copy(w_ref, buf.at[pl.ds(R, R), :], own_sem.at[2])
    own_x.start()
    own_c.start()
    pl.semaphore_wait(barrier, DP + MP - 2)

    def remote(src, dst, send, recv, **to):
        return pltpu.make_async_remote_copy(
            src_ref=src, dst_ref=dst, send_sem=send, recv_sem=recv,
            device_id=to, device_id_type=MESH,
        )

    def taker(s, d):
        return (s + (MP // 2) * (d % 2)) % MP

    def push(d):
        return remote(x_ref.at[:, feat_cols(d)], a_raw.at[rows_of(me), :],
                      in_send.at[d], in_recv.at[me], dp=d)

    def spread(s, q):
        return remote(a_raw.at[rows_of(s), :], a_raw.at[rows_of(s), :],
                      fwd_send.at[s, q], in_recv.at[s], mp=(m + q) % MP)

    def cot_block(zs, lane, j):
        return call.at[rows_of(zs * 2 + lane), cols_of(j)]

    def up(zs, j, src=None):
        dst = cot_block(zs, c, j)
        return remote(dst if src is None else src, dst, up_send.at[zs, j], lane_recv.at[zs, j], dp=(me + 2) % DP)

    def down(zs, j, src=None):
        dst = cot_block(zs, c, j)
        return remote(dst if src is None else src, dst, dn_send.at[zs, j], lane_recv.at[zs, j], dp=(me + DP - 2) % DP)

    def across(zs, j, src=None):
        dst = cot_block(zs, c, j)
        return remote(dst if src is None else src, dst, sib_send.at[zs, j], sib_recv.at[zs, j], dp=sib)

    def across_in(zs, j):
        dst = cot_block(zs, 1 - c, j)
        return remote(dst, dst, sib_send.at[zs, j], sib_recv.at[zs, j], dp=sib)

    def push_step(d, _):
        @pl.when(jnp.logical_and(d != me, taker(me, d) == m))
        def _():
            push(d).start()
        return 0

    lax.fori_loop(0, DP, push_step, 0)

    DEPTH = 3

    def paced(n):
        k, j = n // NC, n % NC

        @pl.when(n >= 0)
        def _():
            @pl.when(jnp.logical_and(z - k >= 0, z < Z - 1))
            def _():
                up(z - k, j).wait_send()

            @pl.when(jnp.logical_and(z + k < Z, z > 0))
            def _():
                down(z + k, j).wait_send()

    def first_send(j, _):
        src = cot_ref.at[:, cols_of(j)]
        paced(j - DEPTH)

        @pl.when(z < Z - 1)
        def _():
            up(z, j, src).start()

        @pl.when(z > 0)
        def _():
            down(z, j, src).start()

        across(z, j, src).start()
        return 0

    def take_step(s, _):
        @pl.when(jnp.logical_and(s != me, taker(s, me) == m))
        def _():
            spread(s, 1).wait_recv()

            def hand(q, _):
                spread(s, q).start()
                return 0

            lax.fori_loop(1, MP, hand, 0)
        return 0

    early = min(5, NC)
    lax.fori_loop(0, early, first_send, 0)
    own_w.start()
    lax.fori_loop(0, DP, take_step, 0)
    lax.fori_loop(early, NC, first_send, 0)

    def relay(k, j):
        lo, hi = z - k, z + k
        paced(k * NC + j - DEPTH)

        @pl.when(lo >= 0)
        def _():
            up(lo, j).wait_recv()

            @pl.when(z < Z - 1)
            def _():
                up(lo, j).start()

            across(lo, j).start()

        @pl.when(hi < Z)
        def _():
            down(hi, j).wait_recv()

            @pl.when(z > 0)
            def _():
                down(hi, j).start()

            across(hi, j).start()

    def weight_step(j, acc):
        relay(1, j)
        v = buf[R:2 * R, cols_of(j)]
        return acc + jnp.sum((v * v).reshape(R // 8, 8, W), axis=0)

    own_w.wait()
    wacc = lax.fori_loop(0, NC, weight_step, jnp.zeros((8, W), F32))
    s_slots[m, 1] = sum(wacc[:, q * LANES:(q + 1) * LANES] for q in range(G))

    def relay_step(i, _):
        relay(2 + i // NC, i % NC)
        return 0

    lax.fori_loop(0, (Z // 2 - 2) * NC, relay_step, 0)

    def rest_step(s, _):
        @pl.when(jnp.logical_and(s != me, taker(s, me) != m))
        def _():
            spread(s, 1).wait_recv()
        return 0

    lax.fori_loop(0, DP, rest_step, 0)
    own_x.wait()
    own_c.wait()

    def turn(i, _):
        cols = pl.ds(pl.multiple_of(i * LANES, LANES), LANES)
        a_t[cols, :] = a_raw[:, cols].T
        return 0

    lax.fori_loop(0, R // LANES, turn, 0)
    row_acc[...] = jnp.zeros_like(row_acc)
    s_acc[...] = jnp.zeros_like(s_acc)

    def col_rows(j):
        return pl.ds(pl.multiple_of(j * G, G), G)

    def col_copy(q, j, own):
        return remote(col_slots.at[own, j], col_slots.at[own, j],
                      col_send.at[q, j], col_recv.at[own, j], dp=(me + q) % DP)

    def s_part(j):
        def got(q, _):
            col_copy(q, j, (me + q) % DP).wait_recv()
            return 0

        lax.fori_loop(1, DP, got, 0)
        tot = lax.fori_loop(1, DP, lambda i, a: a + col_slots[i, j], col_slots[0, j])
        mean = (tot + D * tiny_eps) / D
        inv = []
        for q in range(G):
            row = pl.ds(j * G + q, 1)
            new_cols = decay_rate * cm_ref[row, :] + (1.0 - decay_rate) * mean[q:q + 1, :]
            n_cols[row, :] = new_cols
            inv.append(1.0 / new_cols)

        def s_tile(i, _):
            rows = pl.ds(pl.multiple_of(i * LANES, LANES), LANES)
            part = s_acc[rows, :]
            for q in range(G):
                v = buf[rows, pl.ds(pl.multiple_of(j * W + q * LANES, LANES), LANES)]
                part = part + (v * v) * inv[q]
            s_acc[rows, :] = part
            return 0

        lax.fori_loop(0, RT, s_tile, 0)

    def chunk(j):
        def sib_wait(zs, _):
            @pl.when(zs >= 0)
            def _():
                across_in(zs, j).wait_recv()
            return 0

        lax.fori_loop(0, Z, sib_wait, 0)

        def tile(i, cacc):
            rows = pl.ds(pl.multiple_of(i * BM, BM), BM)
            gt = jnp.dot(a_t[rows, :], call[:, cols_of(j)], preferred_element_type=F32)
            buf[rows, cols_of(j)] = gt
            sq = gt * gt
            row_acc[rows, :] += sum(sq[:, q * LANES:(q + 1) * LANES] for q in range(G))
            return cacc + jnp.sum(sq.reshape(BM // 8, 8, W), axis=0)

        cacc = lax.fori_loop(0, R // BM, tile, jnp.zeros((8, W), F32))
        csum = jnp.sum(cacc, axis=0, keepdims=True)
        for q in range(G):
            col_slots[me, j, q:q + 1, :] = csum[:, q * LANES:(q + 1) * LANES]

        def go(q, _):
            col_copy(q, j, me).start()
            return 0

        lax.fori_loop(1, DP, go, 0)

        @pl.when(j >= LAG)
        def _():
            s_part(j - LAG)

    last = jnp.maximum(z, Z - 1 - z)

    def work_step(i, _):
        k, j = Z // 2 + i // NC, i % NC
        relay(k, j)

        @pl.when(k == last)
        def _():
            chunk(j)
        return 0

    lax.fori_loop(0, (Z - Z // 2) * NC, work_step, 0)

    for i in range(RT):
        block = row_acc[i * LANES:(i + 1) * LANES, :].T
        row_slots[m, i:i + 1, :] = jnp.sum(block, axis=0, keepdims=True)

    def share(slots, send, recv, axis, own, count):
        def go(q, _):
            remote(slots.at[own], slots.at[own], send.at[q], recv.at[own], **{axis: (own + q) % count}).start()
            return 0

        lax.fori_loop(1, count, go, 0)

    def shared(slots, send, recv, axis, own, count):
        def done(q, _):
            src = (own + q) % count
            remote(slots.at[src], slots.at[src], send.at[q], recv.at[src], **{axis: src}).wait_recv()
            return 0

        lax.fori_loop(1, count, done, 0)

    def sent(slots, send, recv, axis, own, count):
        def done(q, _):
            remote(slots.at[own], slots.at[own], send.at[q], recv.at[own], **{axis: (own + q) % count}).wait_send()
            return 0

        lax.fori_loop(1, count, done, 0)

    rows_x = (row_slots, row_send, row_recv, "mp", m, MP)
    s_x = (s_slots, s_send, s_recv, "mp", m, MP)
    t_x = (t_slots, t_send, t_recv, "dp", me, DP)

    def total(slots, count):
        return lax.fori_loop(1, count, lambda i, a: a + slots[i], slots[0])

    share(*rows_x)

    def s_rest(j, _):
        s_part(j)
        return 0

    shared(*rows_x)
    new_rows = decay_rate * rm_ref[...] + (1.0 - decay_rate) * ((total(row_slots, MP) + F * tiny_eps) / F)
    buf[at_rows:at_rows + RT, 0:LANES] = new_rows
    inv_rows = 1.0 / new_rows
    for i in range(RT):
        inv_r[i * LANES:(i + 1) * LANES, :] = jnp.broadcast_to(inv_rows[i:i + 1, :], (LANES, LANES)).T
    lax.fori_loop(NC - LAG, NC, s_rest, 0)
    buf[at_cols:at_cols + CT, 0:LANES] = n_cols[...]

    s_slots[m, 0] = jnp.sum((s_acc[...] * inv_r[...]).reshape(R // 8, 8, LANES), axis=0)
    share(*s_x)
    t_slots[me, 2] = jnp.broadcast_to(jnp.sum(new_rows, axis=0, keepdims=True), (8, LANES))
    shared(*s_x)
    t_slots[me, 0:2] = total(s_slots, MP)
    share(*t_x)

    sent(*rows_x)
    sent(*s_x)

    def push_done(d, _):
        @pl.when(jnp.logical_and(d != me, taker(me, d) == m))
        def _():
            push(d).wait_send()

        @pl.when(jnp.logical_and(d != me, taker(d, me) == m))
        def _():
            def hand(q, _):
                spread(d, q).wait_send()
                return 0

            lax.fori_loop(1, MP, hand, 0)
        return 0

    lax.fori_loop(0, DP, push_done, 0)

    def cot_done(i, _):
        across(i // NC, i % NC).wait_send()
        return 0

    lax.fori_loop(0, Z * NC, cot_done, 0)

    def tail_done(i, _):
        paced(Z * NC - DEPTH + i)
        return 0

    lax.fori_loop(0, DEPTH, tail_done, 0)

    def col_done(i, _):
        col_copy(1 + i // NC, i % NC, me).wait_send()
        return 0

    lax.fori_loop(0, (DP - 1) * NC, col_done, 0)

    shared(*t_x)
    sums = total(t_slots, DP)

    def whole(v):
        return jnp.sum(jnp.sum(v, axis=0, keepdims=True), axis=1, keepdims=True)

    row_mean = whole(sums[2, 0:1, :]) / D
    update_rms = jnp.sqrt(row_mean * whole(sums[0]) / (D * F))
    weight_rms = jnp.sqrt(whole(sums[1]) / (D * F))
    factor = jnp.sqrt(row_mean) / jnp.maximum(1.0, update_rms)
    buf[at_scale:at_scale + 8, 0:LANES] = jnp.broadcast_to(factor, (8, LANES))
    buf[at_scale + 8:at_scale + 16, 0:LANES] = jnp.broadcast_to(step_size * weight_rms, (8, LANES))
    sent(*t_x)


def extras(R, C):
    RT, CT = R // LANES, C // LANES
    at_rows = 2 * R
    at_cols = at_rows + -(-RT // 8) * 8
    return at_rows, at_cols, at_cols + -(-CT // 8) * 8


def apply_kernel(R, C, BR, SLOTS, buf, nw_ref, up_ref, nr_ref, nc_ref, rs, cs, nw_buf, up_buf, nw_sem, up_sem):
    RT, CT = R // LANES, C // LANES
    at_rows, at_cols, at_scale = extras(R, C)
    f1 = buf[at_scale:at_scale + 1, 0:LANES]
    f2 = buf[at_scale + 8:at_scale + 9, 0:LANES]
    new_rows = buf[at_rows:at_rows + RT, 0:LANES]
    new_cols = buf[at_cols:at_cols + CT, 0:LANES]
    nr_ref[...] = new_rows
    nc_ref[...] = new_cols
    cs[...] = lax.rsqrt(new_cols)
    inv = lax.rsqrt(new_rows) * f1
    for i in range(RT):
        rs[i * LANES:(i + 1) * LANES, :] = jnp.broadcast_to(inv[i:i + 1, :], (LANES, LANES)).T
    N = R // BR

    def out_copies(i, slot):
        rows = pl.ds(pl.multiple_of(i * BR, BR), BR)
        return (
            pltpu.make_async_copy(nw_buf.at[slot], nw_ref.at[rows, :], nw_sem.at[slot]),
            pltpu.make_async_copy(up_buf.at[slot], up_ref.at[rows, :], up_sem.at[slot]),
        )

    def step(i, _):
        slot = lax.rem(i, SLOTS)

        @pl.when(i >= SLOTS)
        def _():
            for copy in out_copies(i - SLOTS, slot):
                copy.wait()

        g_rows = pl.ds(pl.multiple_of(i * BR, BR), BR)
        w_rows = pl.ds(pl.multiple_of(R + i * BR, BR), BR)
        scale = rs[g_rows, :]
        for q in range(CT):
            sl = slice(q * LANES, (q + 1) * LANES)
            clipped = buf[g_rows, sl] * (scale * cs[q:q + 1, :])
            nw_buf[slot, :, sl] = buf[w_rows, sl] - f2 * clipped
            up_buf[slot, :, sl] = clipped.astype(up_buf.dtype)
        for copy in out_copies(i, slot):
            copy.start()
        return 0

    lax.fori_loop(0, N, step, 0)

    def drain(i, _):
        for copy in out_copies(i, lax.rem(i, SLOTS)):
            copy.wait()
        return 0

    lax.fori_loop(N - SLOTS, N, drain, 0)


def on_device(MP, DP, inputs, cotangent, weight, row_moment, col_moment):
    T = inputs.shape[0]
    R, C = weight.shape
    Z = DP // 2
    W = min(512, C)
    NC = C // W
    G = W // LANES
    BM = min(512, R)
    RT, CT = R // LANES, C // LANES
    height = extras(R, C)[2] + 16
    vmem = pl.BlockSpec(memory_space=pltpu.VMEM)
    hbm = pl.BlockSpec(memory_space=pl.ANY)
    dma = pltpu.SemaphoreType.DMA
    buf = pl.pallas_call(
        functools.partial(gather_kernel, MP, DP, W, BM, min(4, NC)),
        out_shape=pltpu.VMEM((height, C), F32),
        in_specs=[hbm, hbm, hbm, vmem, vmem],
        out_specs=vmem,
        scratch_shapes=[
            pltpu.VMEM((T * DP, R), jnp.bfloat16),
            pltpu.VMEM((R, T * DP), jnp.bfloat16),
            pltpu.VMEM((T * DP, C), jnp.bfloat16),
            pltpu.VMEM((R, LANES), F32),
            pltpu.VMEM((R, LANES), F32),
            pltpu.VMEM((R, LANES), F32),
            pltpu.VMEM((CT, LANES), F32),
            pltpu.VMEM((MP, RT, LANES), F32),
            pltpu.VMEM((DP, NC, G, LANES), F32),
            pltpu.VMEM((MP, 2, 8, LANES), F32),
            pltpu.VMEM((DP, 3, 8, LANES), F32),
            dma((3,)), dma((DP,)), dma((DP,)), dma((DP, MP)),
            dma((Z, NC)), dma((Z, NC)), dma((Z, NC)), dma((Z, NC)), dma((Z, NC)),
            dma((MP,)), dma((MP,)), dma((DP, NC)), dma((DP, NC)),
            dma((MP,)), dma((MP,)), dma((DP,)), dma((DP,)),
        ],
        compiler_params=pltpu.CompilerParams(
            collective_id=0, has_side_effects=True, vmem_limit_bytes=28 * 2**20
        ),
        cost_estimate=pl.CostEstimate(flops=2 * R * C * T * DP, bytes_accessed=R * C * 4, transcendentals=0),
        name="gather_contract",
    )(inputs, cotangent, weight, row_moment.reshape(RT, LANES), col_moment.reshape(CT, LANES))
    BR = min(64, R)
    SLOTS = min(3, R // BR)
    new_weight, update, nr, nc = pl.pallas_call(
        functools.partial(apply_kernel, R, C, BR, SLOTS),
        out_shape=[
            jax.ShapeDtypeStruct((R, C), F32),
            jax.ShapeDtypeStruct((R, C), jnp.bfloat16),
            jax.ShapeDtypeStruct((RT, LANES), F32),
            jax.ShapeDtypeStruct((CT, LANES), F32),
        ],
        in_specs=[vmem],
        out_specs=[hbm, hbm, vmem, vmem],
        scratch_shapes=[
            pltpu.VMEM((R, LANES), F32),
            pltpu.VMEM((CT, LANES), F32),
            pltpu.VMEM((SLOTS, BR, C), F32),
            pltpu.VMEM((SLOTS, BR, C), jnp.bfloat16),
            dma((SLOTS,)), dma((SLOTS,)),
        ],
        compiler_params=pltpu.CompilerParams(vmem_limit_bytes=16 * 2**20),
        cost_estimate=pl.CostEstimate(flops=4 * R * C, bytes_accessed=R * C * 6, transcendentals=0),
        name="apply_update",
    )(buf)
    return new_weight, update, nr.reshape(R), nc.reshape(C)


def solution(mesh):
    return jax.shard_map(
        functools.partial(on_device, mesh.shape["mp"], mesh.shape["dp"]),
        mesh=mesh,
        in_specs=(P("dp", None), P("dp", "mp"), P("dp", "mp"), P("dp"), P("mp")),
        out_specs=(P("dp", "mp"), P("dp", "mp"), P("dp"), P("mp")),
        check_vma=False,
    )
```

```python
import functools

import jax
import jax.numpy as jnp
from jax import lax
from jax.experimental import pallas as pl
from jax.experimental.pallas import tpu as pltpu
from jax.sharding import PartitionSpec as P

decay_rate = 1.0 - 10.0 ** (-0.8)
step_size = 0.05
tiny_eps = 1e-30

LANES = 128
MESH = pl.DeviceIdType.MESH
F32 = jnp.float32


def gather_kernel(
    MP, DP, W, BM, LAG,
    x_ref, cot_ref, w_ref, rm_ref, cm_ref,
    buf,
    a_raw, a_near, a_far, call, row_acc, s_acc, inv_r, n_cols, row_slots, col_slots, s_slots, t_slots,
    own_sem, own_csem, in_send, in_recv, fwd_send, up_send, dn_send, sib_send,
    lane_recv, sib_recv, row_send, row_recv, col_send, col_recv,
    s_send, s_recv, t_send, t_recv,
):
    m = lax.axis_index("mp")
    me = lax.axis_index("dp")
    z, c = me // 2, me % 2
    Z = DP // 2
    sib = me + 1 - 2 * c
    T = x_ref.shape[0]
    R, C = w_ref.shape
    RT, CT = R // LANES, C // LANES
    NC = C // W
    G = W // LANES
    D, F = R * DP, C * MP
    at_rows, at_cols, at_scale = extras(R, C)

    barrier = pltpu.get_barrier_semaphore()

    def greet_dp(q, _):
        pl.semaphore_signal(barrier, inc=1, device_id={"dp": (me + q) % DP}, device_id_type=MESH)
        return 0

    def greet_mp(q, _):
        pl.semaphore_signal(barrier, inc=1, device_id={"mp": (m + q) % MP}, device_id_type=MESH)
        return 0

    lax.fori_loop(1, DP, greet_dp, 0)
    lax.fori_loop(1, MP, greet_mp, 0)

    def rows_of(s):
        return pl.ds(pl.multiple_of(s * T, T), T)

    def cols_of(j):
        return pl.ds(pl.multiple_of(j * W, W), W)

    def feat_cols(d):
        return pl.ds(pl.multiple_of(d * R, R), R)

    own_x = pltpu.make_async_copy(x_ref.at[:, feat_cols(me)], a_raw.at[rows_of(me), :], own_sem.at[0])
    own_w = pltpu.make_async_copy(w_ref, buf.at[pl.ds(R, R), :], own_sem.at[1])
    own_x.start()

    def own_c(j):
        return pltpu.make_async_copy(cot_ref.at[:, cols_of(j)], call.at[j, rows_of(me), :], own_csem.at[j])

    pl.semaphore_wait(barrier, DP + MP - 2)

    def remote(src, dst, send, recv, **to):
        return pltpu.make_async_remote_copy(
            src_ref=src, dst_ref=dst, send_sem=send, recv_sem=recv,
            device_id=to, device_id_type=MESH,
        )

    def taker(s, d):
        return (s + (MP // 2) * (d % 2)) % MP

    def push(d):
        return remote(x_ref.at[:, feat_cols(d)], a_raw.at[rows_of(me), :],
                      in_send.at[d], in_recv.at[me], dp=d)

    def spread(s, q):
        return remote(a_raw.at[rows_of(s), :], a_raw.at[rows_of(s), :],
                      fwd_send.at[s, q], in_recv.at[s], mp=(m + q) % MP)

    def cot_block(zs, lane, j):
        return call.at[j, rows_of(zs * 2 + lane), :]

    def up(zs, j, src=None):
        dst = cot_block(zs, c, j)
        return remote(dst if src is None else src, dst, up_send.at[zs, j], lane_recv.at[zs, j], dp=(me + 2) % DP)

    def down(zs, j, src=None):
        dst = cot_block(zs, c, j)
        return remote(dst if src is None else src, dst, dn_send.at[zs, j], lane_recv.at[zs, j], dp=(me + DP - 2) % DP)

    def across(zs, j, src=None):
        dst = cot_block(zs, c, j)
        return remote(dst if src is None else src, dst, sib_send.at[zs, j], sib_recv.at[zs, j], dp=sib)

    def across_in(zs, j):
        dst = cot_block(zs, 1 - c, j)
        return remote(dst, dst, sib_send.at[zs, j], sib_recv.at[zs, j], dp=sib)

    def push_step(d, _):
        @pl.when(jnp.logical_and(d != me, taker(me, d) == m))
        def _():
            push(d).start()
        return 0

    lax.fori_loop(0, DP, push_step, 0)

    DEPTH = 6

    def paced(n):
        k, j = n // NC, n % NC

        @pl.when(n >= 0)
        def _():
            @pl.when(jnp.logical_and(z - k >= 0, z < Z - 1))
            def _():
                up(z - k, j).wait_send()

            @pl.when(jnp.logical_and(z + k < Z, z > 0))
            def _():
                down(z + k, j).wait_send()

    def first_send(j, _):
        src = cot_ref.at[:, cols_of(j)]
        paced(j - DEPTH)

        @pl.when(z < Z - 1)
        def _():
            up(z, j, src).start()

        @pl.when(z > 0)
        def _():
            down(z, j, src).start()

        across(z, j, src).start()
        own_c(j).start()
        return 0

    def take_step(s, _):
        @pl.when(jnp.logical_and(s != me, taker(s, me) == m))
        def _():
            spread(s, 1).wait_recv()

            def hand(q, _):
                spread(s, q).start()
                return 0

            lax.fori_loop(1, MP, hand, 0)
        return 0

    early = min(5, NC)
    lax.fori_loop(0, early, first_send, 0)
    own_w.start()
    lax.fori_loop(0, DP, take_step, 0)
    lax.fori_loop(early, NC, first_send, 0)

    def relay(k, j):
        lo, hi = z - k, z + k
        paced(k * NC + j - DEPTH)

        @pl.when(lo >= 0)
        def _():
            up(lo, j).wait_recv()

            @pl.when(z < Z - 1)
            def _():
                up(lo, j).start()

            across(lo, j).start()

        @pl.when(hi < Z)
        def _():
            down(hi, j).wait_recv()

            @pl.when(z > 0)
            def _():
                down(hi, j).start()

            across(hi, j).start()

    def weight_step(j, acc):
        relay(1, j)
        v = buf[R:2 * R, cols_of(j)]
        return acc + jnp.sum((v * v).reshape(R // 8, 8, W), axis=0)

    own_w.wait()
    wacc = lax.fori_loop(0, NC, weight_step, jnp.zeros((8, W), F32))
    s_slots[m, 1] = sum(wacc[:, q * LANES:(q + 1) * LANES] for q in range(G))

    def relay_step(i, _):
        relay(2 + i // NC, i % NC)
        return 0

    lax.fori_loop(0, (Z // 2 - 2) * NC, relay_step, 0)

    def rest_step(s, _):
        @pl.when(jnp.logical_and(s != me, taker(s, me) != m))
        def _():
            spread(s, 1).wait_recv()
        return 0

    lax.fori_loop(0, DP, rest_step, 0)
    own_x.wait()

    def own_done(j, _):
        own_c(j).wait()
        return 0

    lax.fori_loop(0, NC, own_done, 0)

    far_z = jnp.where(z >= Z // 2, 0, Z - 1)
    far_rows = pl.ds(pl.multiple_of(far_z * 2 * T, 2 * T), 2 * T)
    near_rows = pl.ds(pl.multiple_of(jnp.where(z >= Z // 2, 2 * T, 0), 2 * T), (Z - 1) * 2 * T)

    def turn(i, _):
        cols = pl.ds(pl.multiple_of(i * LANES, LANES), LANES)
        a_near[cols, :] = a_raw[near_rows, cols].T
        a_far[cols, :] = a_raw[far_rows, cols].T
        return 0

    lax.fori_loop(0, R // LANES, turn, 0)
    row_acc[...] = jnp.zeros_like(row_acc)
    s_acc[...] = jnp.zeros_like(s_acc)

    def col_rows(j):
        return pl.ds(pl.multiple_of(j * G, G), G)

    def col_copy(q, j, own):
        return remote(col_slots.at[own, j], col_slots.at[own, j],
                      col_send.at[q, j], col_recv.at[own, j], dp=(me + q) % DP)

    def s_part(j):
        def got(q, _):
            col_copy(q, j, (me + q) % DP).wait_recv()
            return 0

        lax.fori_loop(1, DP, got, 0)
        tot = lax.fori_loop(1, DP, lambda i, a: a + col_slots[i, j], col_slots[0, j])
        mean = (tot + D * tiny_eps) / D
        inv = []
        for q in range(G):
            row = pl.ds(j * G + q, 1)
            new_cols = decay_rate * cm_ref[row, :] + (1.0 - decay_rate) * mean[q:q + 1, :]
            n_cols[row, :] = new_cols
            inv.append(1.0 / new_cols)

        def s_tile(i, _):
            rows = pl.ds(pl.multiple_of(i * LANES, LANES), LANES)
            part = s_acc[rows, :]
            for q in range(G):
                v = buf[rows, pl.ds(pl.multiple_of(j * W + q * LANES, LANES), LANES)]
                part = part + (v * v) * inv[q]
            s_acc[rows, :] = part
            return 0

        lax.fori_loop(0, RT, s_tile, 0)

    def near(j):
        def sib_wait(zs, _):
            @pl.when(zs != far_z)
            def _():
                across_in(zs, j).wait_recv()
            return 0

        lax.fori_loop(0, Z, sib_wait, 0)

        def tile(i, _):
            rows = pl.ds(pl.multiple_of(i * BM, BM), BM)
            buf[rows, cols_of(j)] = jnp.dot(a_near[rows, :], call[j, near_rows, :], preferred_element_type=F32)
            return 0

        lax.fori_loop(0, R // BM, tile, 0)

    def chunk(j):
        across_in(far_z, j).wait_recv()

        def tile(i, cacc):
            rows = pl.ds(pl.multiple_of(i * BM, BM), BM)
            gt = buf[rows, cols_of(j)] + jnp.dot(a_far[rows, :], call[j, far_rows, :], preferred_element_type=F32)
            buf[rows, cols_of(j)] = gt
            sq = gt * gt
            row_acc[rows, :] += sum(sq[:, q * LANES:(q + 1) * LANES] for q in range(G))
            return cacc + jnp.sum(sq.reshape(BM // 8, 8, W), axis=0)

        cacc = lax.fori_loop(0, R // BM, tile, jnp.zeros((8, W), F32))
        csum = jnp.sum(cacc, axis=0, keepdims=True)
        for q in range(G):
            col_slots[me, j, q:q + 1, :] = csum[:, q * LANES:(q + 1) * LANES]

        def go(q, _):
            col_copy(q, j, me).start()
            return 0

        lax.fori_loop(1, DP, go, 0)

        @pl.when(j >= LAG)
        def _():
            s_part(j - LAG)

    last = jnp.maximum(z, Z - 1 - z)

    ahead = jnp.where(last == Z - 1, 0, min(2, NC))
    half = (Z // 2) * NC

    def lead_step(i, _):
        relay(Z // 2 + i // NC, i % NC)
        return 0

    lax.fori_loop(0, ahead, lead_step, 0)

    def work_step(i, _):
        j = i % NC
        mine = Z // 2 + i // NC == last

        @pl.when(mine)
        def _():
            near(j)

        @pl.when(i + ahead < Z * NC - half)
        def _():
            relay(Z // 2 + (i + ahead) // NC, (i + ahead) % NC)

        @pl.when(mine)
        def _():
            chunk(j)
        return 0

    lax.fori_loop(0, Z * NC - half, work_step, 0)

    for i in range(RT):
        block = row_acc[i * LANES:(i + 1) * LANES, :].T
        row_slots[m, i:i + 1, :] = jnp.sum(block, axis=0, keepdims=True)

    def share(slots, send, recv, axis, own, count):
        def go(q, _):
            remote(slots.at[own], slots.at[own], send.at[q], recv.at[own], **{axis: (own + q) % count}).start()
            return 0

        lax.fori_loop(1, count, go, 0)

    def shared(slots, send, recv, axis, own, count):
        def done(q, _):
            src = (own + q) % count
            remote(slots.at[src], slots.at[src], send.at[q], recv.at[src], **{axis: src}).wait_recv()
            return 0

        lax.fori_loop(1, count, done, 0)

    def sent(slots, send, recv, axis, own, count):
        def done(q, _):
            remote(slots.at[own], slots.at[own], send.at[q], recv.at[own], **{axis: (own + q) % count}).wait_send()
            return 0

        lax.fori_loop(1, count, done, 0)

    rows_x = (row_slots, row_send, row_recv, "mp", m, MP)
    s_x = (s_slots, s_send, s_recv, "mp", m, MP)
    t_x = (t_slots, t_send, t_recv, "dp", me, DP)

    def total(slots, count):
        return lax.fori_loop(1, count, lambda i, a: a + slots[i], slots[0])

    share(*rows_x)

    def s_rest(j, _):
        s_part(j)
        return 0

    shared(*rows_x)
    new_rows = decay_rate * rm_ref[...] + (1.0 - decay_rate) * ((total(row_slots, MP) + F * tiny_eps) / F)
    buf[at_rows:at_rows + RT, 0:LANES] = new_rows
    inv_rows = 1.0 / new_rows
    for i in range(RT):
        inv_r[i * LANES:(i + 1) * LANES, :] = jnp.broadcast_to(inv_rows[i:i + 1, :], (LANES, LANES)).T
    lax.fori_loop(NC - LAG, NC, s_rest, 0)
    buf[at_cols:at_cols + CT, 0:LANES] = n_cols[...]

    s_slots[m, 0] = jnp.sum((s_acc[...] * inv_r[...]).reshape(R // 8, 8, LANES), axis=0)
    share(*s_x)
    t_slots[me, 2] = jnp.broadcast_to(jnp.sum(new_rows, axis=0, keepdims=True), (8, LANES))
    shared(*s_x)
    t_slots[me, 0:2] = total(s_slots, MP)
    share(*t_x)

    sent(*rows_x)
    sent(*s_x)

    def push_done(d, _):
        @pl.when(jnp.logical_and(d != me, taker(me, d) == m))
        def _():
            push(d).wait_send()

        @pl.when(jnp.logical_and(d != me, taker(d, me) == m))
        def _():
            def hand(q, _):
                spread(d, q).wait_send()
                return 0

            lax.fori_loop(1, MP, hand, 0)
        return 0

    lax.fori_loop(0, DP, push_done, 0)

    def cot_done(i, _):
        across(i // NC, i % NC).wait_send()
        return 0

    lax.fori_loop(0, Z * NC, cot_done, 0)

    def tail_done(i, _):
        paced(Z * NC - DEPTH + i)
        return 0

    lax.fori_loop(0, DEPTH, tail_done, 0)

    def col_done(i, _):
        col_copy(1 + i // NC, i % NC, me).wait_send()
        return 0

    lax.fori_loop(0, (DP - 1) * NC, col_done, 0)

    shared(*t_x)
    sums = total(t_slots, DP)

    def whole(v):
        return jnp.sum(jnp.sum(v, axis=0, keepdims=True), axis=1, keepdims=True)

    row_mean = whole(sums[2, 0:1, :]) / D
    update_rms = jnp.sqrt(row_mean * whole(sums[0]) / (D * F))
    weight_rms = jnp.sqrt(whole(sums[1]) / (D * F))
    factor = jnp.sqrt(row_mean) / jnp.maximum(1.0, update_rms)
    buf[at_scale:at_scale + 8, 0:LANES] = jnp.broadcast_to(factor, (8, LANES))
    buf[at_scale + 8:at_scale + 16, 0:LANES] = jnp.broadcast_to(step_size * weight_rms, (8, LANES))
    sent(*t_x)


def extras(R, C):
    RT, CT = R // LANES, C // LANES
    at_rows = 2 * R
    at_cols = at_rows + -(-RT // 8) * 8
    return at_rows, at_cols, at_cols + -(-CT // 8) * 8


def apply_kernel(R, C, BR, SLOTS, buf, nw_ref, up_ref, nr_ref, nc_ref, rs, cs, nw_buf, up_buf, nw_sem, up_sem):
    RT, CT = R // LANES, C // LANES
    at_rows, at_cols, at_scale = extras(R, C)
    f1 = buf[at_scale:at_scale + 1, 0:LANES]
    f2 = buf[at_scale + 8:at_scale + 9, 0:LANES]
    new_rows = buf[at_rows:at_rows + RT, 0:LANES]
    new_cols = buf[at_cols:at_cols + CT, 0:LANES]
    nr_ref[...] = new_rows
    nc_ref[...] = new_cols
    cs[...] = lax.rsqrt(new_cols)
    inv = lax.rsqrt(new_rows) * f1
    for i in range(RT):
        rs[i * LANES:(i + 1) * LANES, :] = jnp.broadcast_to(inv[i:i + 1, :], (LANES, LANES)).T
    N = R // BR

    def out_copies(i, slot):
        rows = pl.ds(pl.multiple_of(i * BR, BR), BR)
        return (
            pltpu.make_async_copy(nw_buf.at[slot], nw_ref.at[rows, :], nw_sem.at[slot]),
            pltpu.make_async_copy(up_buf.at[slot], up_ref.at[rows, :], up_sem.at[slot]),
        )

    def step(i, _):
        slot = lax.rem(i, SLOTS)

        @pl.when(i >= SLOTS)
        def _():
            for copy in out_copies(i - SLOTS, slot):
                copy.wait()

        g_rows = pl.ds(pl.multiple_of(i * BR, BR), BR)
        w_rows = pl.ds(pl.multiple_of(R + i * BR, BR), BR)
        scale = rs[g_rows, :]
        for q in range(CT):
            sl = slice(q * LANES, (q + 1) * LANES)
            clipped = buf[g_rows, sl] * (scale * cs[q:q + 1, :])
            nw_buf[slot, :, sl] = buf[w_rows, sl] - f2 * clipped
            up_buf[slot, :, sl] = clipped.astype(up_buf.dtype)
        for copy in out_copies(i, slot):
            copy.start()
        return 0

    lax.fori_loop(0, N, step, 0)

    def drain(i, _):
        for copy in out_copies(i, lax.rem(i, SLOTS)):
            copy.wait()
        return 0

    lax.fori_loop(N - SLOTS, N, drain, 0)


def on_device(MP, DP, inputs, cotangent, weight, row_moment, col_moment):
    T = inputs.shape[0]
    R, C = weight.shape
    Z = DP // 2
    W = min(512, C)
    NC = C // W
    G = W // LANES
    BM = min(512, R)
    RT, CT = R // LANES, C // LANES
    height = extras(R, C)[2] + 16
    vmem = pl.BlockSpec(memory_space=pltpu.VMEM)
    hbm = pl.BlockSpec(memory_space=pl.ANY)
    dma = pltpu.SemaphoreType.DMA
    buf = pl.pallas_call(
        functools.partial(gather_kernel, MP, DP, W, BM, min(3, NC)),
        out_shape=pltpu.VMEM((height, C), F32),
        in_specs=[hbm, hbm, hbm, vmem, vmem],
        out_specs=vmem,
        scratch_shapes=[
            pltpu.VMEM((T * DP, R), jnp.bfloat16),
            pltpu.VMEM((R, T * (DP - 2)), jnp.bfloat16),
            pltpu.VMEM((R, 2 * T), jnp.bfloat16),
            pltpu.VMEM((NC, T * DP, W), jnp.bfloat16),
            pltpu.VMEM((R, LANES), F32),
            pltpu.VMEM((R, LANES), F32),
            pltpu.VMEM((R, LANES), F32),
            pltpu.VMEM((CT, LANES), F32),
            pltpu.VMEM((MP, RT, LANES), F32),
            pltpu.VMEM((DP, NC, G, LANES), F32),
            pltpu.VMEM((MP, 2, 8, LANES), F32),
            pltpu.VMEM((DP, 3, 8, LANES), F32),
            dma((2,)), dma((NC,)), dma((DP,)), dma((DP,)), dma((DP, MP)),
            dma((Z, NC)), dma((Z, NC)), dma((Z, NC)), dma((Z, NC)), dma((Z, NC)),
            dma((MP,)), dma((MP,)), dma((DP, NC)), dma((DP, NC)),
            dma((MP,)), dma((MP,)), dma((DP,)), dma((DP,)),
        ],
        compiler_params=pltpu.CompilerParams(
            collective_id=0, has_side_effects=True, vmem_limit_bytes=28 * 2**20
        ),
        cost_estimate=pl.CostEstimate(flops=2 * R * C * T * DP, bytes_accessed=R * C * 4, transcendentals=0),
        name="gather_contract",
    )(inputs, cotangent, weight, row_moment.reshape(RT, LANES), col_moment.reshape(CT, LANES))
    BR = min(64, R)
    SLOTS = min(3, R // BR)
    new_weight, update, nr, nc = pl.pallas_call(
        functools.partial(apply_kernel, R, C, BR, SLOTS),
        out_shape=[
            jax.ShapeDtypeStruct((R, C), F32),
            jax.ShapeDtypeStruct((R, C), jnp.bfloat16),
            jax.ShapeDtypeStruct((RT, LANES), F32),
            jax.ShapeDtypeStruct((CT, LANES), F32),
        ],
        in_specs=[vmem],
        out_specs=[hbm, hbm, vmem, vmem],
        scratch_shapes=[
            pltpu.VMEM((R, LANES), F32),
            pltpu.VMEM((CT, LANES), F32),
            pltpu.VMEM((SLOTS, BR, C), F32),
            pltpu.VMEM((SLOTS, BR, C), jnp.bfloat16),
            dma((SLOTS,)), dma((SLOTS,)),
        ],
        compiler_params=pltpu.CompilerParams(vmem_limit_bytes=16 * 2**20),
        cost_estimate=pl.CostEstimate(flops=4 * R * C, bytes_accessed=R * C * 6, transcendentals=0),
        name="apply_update",
    )(buf)
    return new_weight, update, nr.reshape(R), nc.reshape(C)


def solution(mesh):
    return jax.shard_map(
        functools.partial(on_device, mesh.shape["mp"], mesh.shape["dp"]),
        mesh=mesh,
        in_specs=(P("dp", None), P("dp", "mp"), P("dp", "mp"), P("dp"), P("mp")),
        out_specs=(P("dp", "mp"), P("dp", "mp"), P("dp"), P("mp")),
        check_vma=False,
    )
```

```python
import functools

import jax
import jax.numpy as jnp
from jax import lax
from jax.experimental import pallas as pl
from jax.experimental.pallas import tpu as pltpu
from jax.sharding import PartitionSpec as P

decay_rate = 1.0 - 10.0 ** (-0.8)
step_size = 0.05
tiny_eps = 1e-30

LANES = 128
MESH = pl.DeviceIdType.MESH
F32 = jnp.float32


def gather_kernel(
    MP, DP, W, BM, LAG,
    x_ref, cot_ref, w_ref, rm_ref, cm_ref,
    buf,
    a_raw, a_t, call, row_acc, s_acc, inv_r, n_cols, row_slots, col_slots, s_slots, t_slots,
    own_sem, in_send, in_recv, fwd_send, up_send, dn_send, sib_send,
    lane_recv, sib_recv, row_send, row_recv, col_send, col_recv,
    s_send, s_recv, t_send, t_recv,
):
    m = lax.axis_index("mp")
    me = lax.axis_index("dp")
    z, c = me // 2, me % 2
    Z = DP // 2
    sib = me + 1 - 2 * c
    T = x_ref.shape[0]
    R, C = w_ref.shape
    RT, CT = R // LANES, C // LANES
    NC = C // W
    G = W // LANES
    D, F = R * DP, C * MP
    at_rows, at_cols, at_scale = extras(R, C)

    barrier = pltpu.get_barrier_semaphore()

    def greet_dp(q, _):
        pl.semaphore_signal(barrier, inc=1, device_id={"dp": (me + q) % DP}, device_id_type=MESH)
        return 0

    def greet_mp(q, _):
        pl.semaphore_signal(barrier, inc=1, device_id={"mp": (m + q) % MP}, device_id_type=MESH)
        return 0

    lax.fori_loop(1, DP, greet_dp, 0)
    lax.fori_loop(1, MP, greet_mp, 0)

    def rows_of(s):
        return pl.ds(pl.multiple_of(s * T, T), T)

    def cols_of(j):
        return pl.ds(pl.multiple_of(j * W, W), W)

    def feat_cols(d):
        return pl.ds(pl.multiple_of(d * R, R), R)

    own_x = pltpu.make_async_copy(x_ref.at[:, feat_cols(me)], a_raw.at[rows_of(me), :], own_sem.at[0])
    own_c = pltpu.make_async_copy(cot_ref, call.at[rows_of(me), :], own_sem.at[1])
    own_w = pltpu.make_async_copy(w_ref, buf.at[pl.ds(R, R), :], own_sem.at[2])
    own_x.start()
    own_c.start()
    pl.semaphore_wait(barrier, DP + MP - 2)

    def remote(src, dst, send, recv, **to):
        return pltpu.make_async_remote_copy(
            src_ref=src, dst_ref=dst, send_sem=send, recv_sem=recv,
            device_id=to, device_id_type=MESH,
        )

    def taker(s, d):
        return (s + (MP // 2) * (d % 2)) % MP

    def push(d):
        return remote(x_ref.at[:, feat_cols(d)], a_raw.at[rows_of(me), :],
                      in_send.at[d], in_recv.at[me], dp=d)

    def spread(s, q):
        return remote(a_raw.at[rows_of(s), :], a_raw.at[rows_of(s), :],
                      fwd_send.at[s, q], in_recv.at[s], mp=(m + q) % MP)

    def cot_block(zs, lane, j):
        return call.at[rows_of(zs * 2 + lane), cols_of(j)]

    def up(zs, j, src=None):
        dst = cot_block(zs, c, j)
        return remote(dst if src is None else src, dst, up_send.at[zs, j], lane_recv.at[zs, j], dp=(me + 2) % DP)

    def down(zs, j, src=None):
        dst = cot_block(zs, c, j)
        return remote(dst if src is None else src, dst, dn_send.at[zs, j], lane_recv.at[zs, j], dp=(me + DP - 2) % DP)

    def across(zs, j, src=None):
        dst = cot_block(zs, c, j)
        return remote(dst if src is None else src, dst, sib_send.at[zs, j], sib_recv.at[zs, j], dp=sib)

    def across_in(zs, j):
        dst = cot_block(zs, 1 - c, j)
        return remote(dst, dst, sib_send.at[zs, j], sib_recv.at[zs, j], dp=sib)

    def push_step(d, _):
        @pl.when(jnp.logical_and(d != me, taker(me, d) == m))
        def _():
            push(d).start()
        return 0

    lax.fori_loop(0, DP, push_step, 0)

    DEPTH = 3

    def paced(n):
        k, j = n // NC, n % NC

        @pl.when(n >= 0)
        def _():
            @pl.when(jnp.logical_and(z - k >= 0, z < Z - 1))
            def _():
                up(z - k, j).wait_send()

            @pl.when(jnp.logical_and(z + k < Z, z > 0))
            def _():
                down(z + k, j).wait_send()

    def first_send(j, _):
        src = cot_ref.at[:, cols_of(j)]
        paced(j - DEPTH)

        @pl.when(z < Z - 1)
        def _():
            up(z, j, src).start()

        @pl.when(z > 0)
        def _():
            down(z, j, src).start()

        across(z, j, src).start()
        return 0

    def take_step(s, _):
        @pl.when(jnp.logical_and(s != me, taker(s, me) == m))
        def _():
            spread(s, 1).wait_recv()

            def hand(q, _):
                spread(s, q).start()
                return 0

            lax.fori_loop(1, MP, hand, 0)
        return 0

    early = min(5, NC)
    lax.fori_loop(0, early, first_send, 0)
    own_w.start()
    lax.fori_loop(0, DP, take_step, 0)
    lax.fori_loop(early, NC, first_send, 0)

    def relay(k, j):
        lo, hi = z - k, z + k
        paced(k * NC + j - DEPTH)

        @pl.when(lo >= 0)
        def _():
            up(lo, j).wait_recv()

            @pl.when(z < Z - 1)
            def _():
                up(lo, j).start()

            across(lo, j).start()

        @pl.when(hi < Z)
        def _():
            down(hi, j).wait_recv()

            @pl.when(z > 0)
            def _():
                down(hi, j).start()

            across(hi, j).start()

    def weight_step(j, acc):
        relay(1, j)
        v = buf[R:2 * R, cols_of(j)]
        return acc + jnp.sum((v * v).reshape(R // 8, 8, W), axis=0)

    own_w.wait()
    wacc = lax.fori_loop(0, NC, weight_step, jnp.zeros((8, W), F32))
    s_slots[m, 1] = sum(wacc[:, q * LANES:(q + 1) * LANES] for q in range(G))

    def relay_step(i, _):
        relay(2 + i // NC, i % NC)
        return 0

    lax.fori_loop(0, (Z - 4) * NC, relay_step, 0)

    def rest_step(s, _):
        @pl.when(jnp.logical_and(s != me, taker(s, me) != m))
        def _():
            spread(s, 1).wait_recv()
        return 0

    lax.fori_loop(0, DP, rest_step, 0)
    own_x.wait()
    own_c.wait()

    def turn(i, _):
        cols = pl.ds(pl.multiple_of(i * LANES, LANES), LANES)
        a_t[cols, :] = a_raw[:, cols].T
        return 0

    lax.fori_loop(0, R // LANES, turn, 0)
    row_acc[...] = jnp.zeros_like(row_acc)
    s_acc[...] = jnp.zeros_like(s_acc)

    def col_rows(j):
        return pl.ds(pl.multiple_of(j * G, G), G)

    def col_copy(q, j, own):
        return remote(col_slots.at[own, j], col_slots.at[own, j],
                      col_send.at[q, j], col_recv.at[own, j], dp=(me + q) % DP)

    def s_part(j):
        def got(q, _):
            col_copy(q, j, (me + q) % DP).wait_recv()
            return 0

        lax.fori_loop(1, DP, got, 0)
        tot = lax.fori_loop(1, DP, lambda i, a: a + col_slots[i, j], col_slots[0, j])
        mean = (tot + D * tiny_eps) / D
        inv = []
        for q in range(G):
            row = pl.ds(j * G + q, 1)
            new_cols = decay_rate * cm_ref[row, :] + (1.0 - decay_rate) * mean[q:q + 1, :]
            n_cols[row, :] = new_cols
            inv.append(1.0 / new_cols)

        def s_tile(i, _):
            rows = pl.ds(pl.multiple_of(i * LANES, LANES), LANES)
            part = s_acc[rows, :]
            for q in range(G):
                v = buf[rows, pl.ds(pl.multiple_of(j * W + q * LANES, LANES), LANES)]
                part = part + (v * v) * inv[q]
            s_acc[rows, :] = part
            return 0

        lax.fori_loop(0, RT, s_tile, 0)

    half = Z // 2 * 2 * T
    mine = z // (Z // 2)

    def tokens(h):
        return pl.ds(pl.multiple_of(h * half, half), half)

    def sib_wait(h, j):
        def wait(i, _):
            across_in(h * (Z // 2) + i, j).wait_recv()
            return 0

        lax.fori_loop(0, Z // 2, wait, 0)

    def first_half(j):
        sib_wait(mine, j)

        def tile(i, _):
            rows = pl.ds(pl.multiple_of(i * BM, BM), BM)
            buf[rows, cols_of(j)] = jnp.dot(
                a_t[rows, tokens(mine)], call[tokens(mine), cols_of(j)], preferred_element_type=F32
            )
            return 0

        lax.fori_loop(0, R // BM, tile, 0)

    def chunk(j):
        sib_wait(1 - mine, j)

        def tile(i, cacc):
            rows = pl.ds(pl.multiple_of(i * BM, BM), BM)
            gt = buf[rows, cols_of(j)] + jnp.dot(
                a_t[rows, tokens(1 - mine)], call[tokens(1 - mine), cols_of(j)], preferred_element_type=F32
            )
            buf[rows, cols_of(j)] = gt
            sq = gt * gt
            row_acc[rows, :] += sum(sq[:, q * LANES:(q + 1) * LANES] for q in range(G))
            return cacc + jnp.sum(sq.reshape(BM // 8, 8, W), axis=0)

        cacc = lax.fori_loop(0, R // BM, tile, jnp.zeros((8, W), F32))
        csum = jnp.sum(cacc, axis=0, keepdims=True)
        for q in range(G):
            col_slots[me, j, q:q + 1, :] = csum[:, q * LANES:(q + 1) * LANES]

        def go(q, _):
            col_copy(q, j, me).start()
            return 0

        lax.fori_loop(1, DP, go, 0)

        @pl.when(j >= LAG)
        def _():
            s_part(j - LAG)

    def first_step(j, _):
        relay(Z - 2, j)
        first_half(j)
        return 0

    def last_step(j, _):
        relay(Z - 1, j)
        chunk(j)
        return 0

    lax.fori_loop(0, NC, first_step, 0)
    lax.fori_loop(0, NC, last_step, 0)

    for i in range(RT):
        block = row_acc[i * LANES:(i + 1) * LANES, :].T
        row_slots[m, i:i + 1, :] = jnp.sum(block, axis=0, keepdims=True)

    def share(slots, send, recv, axis, own, count):
        def go(q, _):
            remote(slots.at[own], slots.at[own], send.at[q], recv.at[own], **{axis: (own + q) % count}).start()
            return 0

        lax.fori_loop(1, count, go, 0)

    def shared(slots, send, recv, axis, own, count):
        def done(q, _):
            src = (own + q) % count
            remote(slots.at[src], slots.at[src], send.at[q], recv.at[src], **{axis: src}).wait_recv()
            return 0

        lax.fori_loop(1, count, done, 0)

    def sent(slots, send, recv, axis, own, count):
        def done(q, _):
            remote(slots.at[own], slots.at[own], send.at[q], recv.at[own], **{axis: (own + q) % count}).wait_send()
            return 0

        lax.fori_loop(1, count, done, 0)

    rows_x = (row_slots, row_send, row_recv, "mp", m, MP)
    s_x = (s_slots, s_send, s_recv, "mp", m, MP)
    t_x = (t_slots, t_send, t_recv, "dp", me, DP)

    def total(slots, count):
        return lax.fori_loop(1, count, lambda i, a: a + slots[i], slots[0])

    share(*rows_x)

    def s_rest(j, _):
        s_part(j)
        return 0

    shared(*rows_x)
    new_rows = decay_rate * rm_ref[...] + (1.0 - decay_rate) * ((total(row_slots, MP) + F * tiny_eps) / F)
    buf[at_rows:at_rows + RT, 0:LANES] = new_rows
    inv_rows = 1.0 / new_rows
    for i in range(RT):
        inv_r[i * LANES:(i + 1) * LANES, :] = jnp.broadcast_to(inv_rows[i:i + 1, :], (LANES, LANES)).T
    lax.fori_loop(NC - LAG, NC, s_rest, 0)
    buf[at_cols:at_cols + CT, 0:LANES] = n_cols[...]

    s_slots[m, 0] = jnp.sum((s_acc[...] * inv_r[...]).reshape(R // 8, 8, LANES), axis=0)
    share(*s_x)
    t_slots[me, 2] = jnp.broadcast_to(jnp.sum(new_rows, axis=0, keepdims=True), (8, LANES))
    shared(*s_x)
    t_slots[me, 0:2] = total(s_slots, MP)
    share(*t_x)

    sent(*rows_x)
    sent(*s_x)

    def push_done(d, _):
        @pl.when(jnp.logical_and(d != me, taker(me, d) == m))
        def _():
            push(d).wait_send()

        @pl.when(jnp.logical_and(d != me, taker(d, me) == m))
        def _():
            def hand(q, _):
                spread(d, q).wait_send()
                return 0

            lax.fori_loop(1, MP, hand, 0)
        return 0

    lax.fori_loop(0, DP, push_done, 0)

    def cot_done(i, _):
        across(i // NC, i % NC).wait_send()
        return 0

    lax.fori_loop(0, Z * NC, cot_done, 0)

    def tail_done(i, _):
        paced(Z * NC - DEPTH + i)
        return 0

    lax.fori_loop(0, DEPTH, tail_done, 0)

    def col_done(i, _):
        col_copy(1 + i // NC, i % NC, me).wait_send()
        return 0

    lax.fori_loop(0, (DP - 1) * NC, col_done, 0)

    shared(*t_x)
    sums = total(t_slots, DP)

    def whole(v):
        return jnp.sum(jnp.sum(v, axis=0, keepdims=True), axis=1, keepdims=True)

    row_mean = whole(sums[2, 0:1, :]) / D
    update_rms = jnp.sqrt(row_mean * whole(sums[0]) / (D * F))
    weight_rms = jnp.sqrt(whole(sums[1]) / (D * F))
    factor = jnp.sqrt(row_mean) / jnp.maximum(1.0, update_rms)
    buf[at_scale:at_scale + 8, 0:LANES] = jnp.broadcast_to(factor, (8, LANES))
    buf[at_scale + 8:at_scale + 16, 0:LANES] = jnp.broadcast_to(step_size * weight_rms, (8, LANES))
    sent(*t_x)


def extras(R, C):
    RT, CT = R // LANES, C // LANES
    at_rows = 2 * R
    at_cols = at_rows + -(-RT // 8) * 8
    return at_rows, at_cols, at_cols + -(-CT // 8) * 8


def apply_kernel(R, C, BR, SLOTS, buf, nw_ref, up_ref, nr_ref, nc_ref, rs, cs, nw_buf, up_buf, nw_sem, up_sem):
    RT, CT = R // LANES, C // LANES
    at_rows, at_cols, at_scale = extras(R, C)
    f1 = buf[at_scale:at_scale + 1, 0:LANES]
    f2 = buf[at_scale + 8:at_scale + 9, 0:LANES]
    new_rows = buf[at_rows:at_rows + RT, 0:LANES]
    new_cols = buf[at_cols:at_cols + CT, 0:LANES]
    nr_ref[...] = new_rows
    nc_ref[...] = new_cols
    cs[...] = lax.rsqrt(new_cols)
    inv = lax.rsqrt(new_rows) * f1
    for i in range(RT):
        rs[i * LANES:(i + 1) * LANES, :] = jnp.broadcast_to(inv[i:i + 1, :], (LANES, LANES)).T
    N = R // BR

    def out_copies(i, slot):
        rows = pl.ds(pl.multiple_of(i * BR, BR), BR)
        return (
            pltpu.make_async_copy(nw_buf.at[slot], nw_ref.at[rows, :], nw_sem.at[slot]),
            pltpu.make_async_copy(up_buf.at[slot], up_ref.at[rows, :], up_sem.at[slot]),
        )

    def step(i, _):
        slot = lax.rem(i, SLOTS)

        @pl.when(i >= SLOTS)
        def _():
            for copy in out_copies(i - SLOTS, slot):
                copy.wait()

        g_rows = pl.ds(pl.multiple_of(i * BR, BR), BR)
        w_rows = pl.ds(pl.multiple_of(R + i * BR, BR), BR)
        scale = rs[g_rows, :]
        for q in range(CT):
            sl = slice(q * LANES, (q + 1) * LANES)
            clipped = buf[g_rows, sl] * (scale * cs[q:q + 1, :])
            nw_buf[slot, :, sl] = buf[w_rows, sl] - f2 * clipped
            up_buf[slot, :, sl] = clipped.astype(up_buf.dtype)
        for copy in out_copies(i, slot):
            copy.start()
        return 0

    lax.fori_loop(0, N, step, 0)

    def drain(i, _):
        for copy in out_copies(i, lax.rem(i, SLOTS)):
            copy.wait()
        return 0

    lax.fori_loop(N - SLOTS, N, drain, 0)


def on_device(MP, DP, inputs, cotangent, weight, row_moment, col_moment):
    T = inputs.shape[0]
    R, C = weight.shape
    Z = DP // 2
    W = min(512, C)
    NC = C // W
    G = W // LANES
    BM = min(512, R)
    RT, CT = R // LANES, C // LANES
    height = extras(R, C)[2] + 16
    vmem = pl.BlockSpec(memory_space=pltpu.VMEM)
    hbm = pl.BlockSpec(memory_space=pl.ANY)
    dma = pltpu.SemaphoreType.DMA
    buf = pl.pallas_call(
        functools.partial(gather_kernel, MP, DP, W, BM, min(3, NC)),
        out_shape=pltpu.VMEM((height, C), F32),
        in_specs=[hbm, hbm, hbm, vmem, vmem],
        out_specs=vmem,
        scratch_shapes=[
            pltpu.VMEM((T * DP, R), jnp.bfloat16),
            pltpu.VMEM((R, T * DP), jnp.bfloat16),
            pltpu.VMEM((T * DP, C), jnp.bfloat16),
            pltpu.VMEM((R, LANES), F32),
            pltpu.VMEM((R, LANES), F32),
            pltpu.VMEM((R, LANES), F32),
            pltpu.VMEM((CT, LANES), F32),
            pltpu.VMEM((MP, RT, LANES), F32),
            pltpu.VMEM((DP, NC, G, LANES), F32),
            pltpu.VMEM((MP, 2, 8, LANES), F32),
            pltpu.VMEM((DP, 3, 8, LANES), F32),
            dma((3,)), dma((DP,)), dma((DP,)), dma((DP, MP)),
            dma((Z, NC)), dma((Z, NC)), dma((Z, NC)), dma((Z, NC)), dma((Z, NC)),
            dma((MP,)), dma((MP,)), dma((DP, NC)), dma((DP, NC)),
            dma((MP,)), dma((MP,)), dma((DP,)), dma((DP,)),
        ],
        compiler_params=pltpu.CompilerParams(
            collective_id=0, has_side_effects=True, vmem_limit_bytes=28 * 2**20
        ),
        cost_estimate=pl.CostEstimate(flops=2 * R * C * T * DP, bytes_accessed=R * C * 4, transcendentals=0),
        name="gather_contract",
    )(inputs, cotangent, weight, row_moment.reshape(RT, LANES), col_moment.reshape(CT, LANES))
    BR = min(64, R)
    SLOTS = min(3, R // BR)
    new_weight, update, nr, nc = pl.pallas_call(
        functools.partial(apply_kernel, R, C, BR, SLOTS),
        out_shape=[
            jax.ShapeDtypeStruct((R, C), F32),
            jax.ShapeDtypeStruct((R, C), jnp.bfloat16),
            jax.ShapeDtypeStruct((RT, LANES), F32),
            jax.ShapeDtypeStruct((CT, LANES), F32),
        ],
        in_specs=[vmem],
        out_specs=[hbm, hbm, vmem, vmem],
        scratch_shapes=[
            pltpu.VMEM((R, LANES), F32),
            pltpu.VMEM((CT, LANES), F32),
            pltpu.VMEM((SLOTS, BR, C), F32),
            pltpu.VMEM((SLOTS, BR, C), jnp.bfloat16),
            dma((SLOTS,)), dma((SLOTS,)),
        ],
        compiler_params=pltpu.CompilerParams(vmem_limit_bytes=16 * 2**20),
        cost_estimate=pl.CostEstimate(flops=4 * R * C, bytes_accessed=R * C * 6, transcendentals=0),
        name="apply_update",
    )(buf)
    return new_weight, update, nr.reshape(R), nc.reshape(C)


def solution(mesh):
    return jax.shard_map(
        functools.partial(on_device, mesh.shape["mp"], mesh.shape["dp"]),
        mesh=mesh,
        in_specs=(P("dp", None), P("dp", "mp"), P("dp", "mp"), P("dp"), P("mp")),
        out_specs=(P("dp", "mp"), P("dp", "mp"), P("dp"), P("mp")),
        check_vma=False,
    )
```

```python
import functools

import jax
import jax.numpy as jnp
from jax import lax
from jax.experimental import pallas as pl
from jax.experimental.pallas import tpu as pltpu
from jax.sharding import PartitionSpec as P

decay_rate = 1.0 - 10.0 ** (-0.8)
step_size = 0.05
tiny_eps = 1e-30

LANES = 128
MESH = pl.DeviceIdType.MESH
F32 = jnp.float32


def gather_kernel(
    MP, DP, W, BM, LAG, EARLY,
    x_ref, cot_ref, w_ref, rm_ref, cm_ref,
    buf,
    a_raw, a_t, call, row_acc, s_acc, inv_r, n_cols, row_slots, col_slots, s_slots, t_slots,
    own_sem, in_send, in_recv, fwd_send, up_send, dn_send, sib_send,
    lane_recv, sib_recv, row_send, row_recv, col_send, col_recv,
    s_send, s_recv, t_send, t_recv,
):
    m = lax.axis_index("mp")
    me = lax.axis_index("dp")
    z, c = me // 2, me % 2
    Z = DP // 2
    sib = me + 1 - 2 * c
    T = x_ref.shape[0]
    R, C = w_ref.shape
    RT, CT = R // LANES, C // LANES
    NC = C // W
    G = W // LANES
    D, F = R * DP, C * MP
    at_rows, at_cols, at_scale = extras(R, C)

    barrier = pltpu.get_barrier_semaphore()

    def greet_dp(q, _):
        pl.semaphore_signal(barrier, inc=1, device_id={"dp": (me + q) % DP}, device_id_type=MESH)
        return 0

    def greet_mp(q, _):
        pl.semaphore_signal(barrier, inc=1, device_id={"mp": (m + q) % MP}, device_id_type=MESH)
        return 0

    lax.fori_loop(1, DP, greet_dp, 0)
    lax.fori_loop(1, MP, greet_mp, 0)

    def rows_of(s):
        return pl.ds(pl.multiple_of(s * T, T), T)

    def cols_of(j):
        return pl.ds(pl.multiple_of(j * W, W), W)

    def feat_cols(d):
        return pl.ds(pl.multiple_of(d * R, R), R)

    own_x = pltpu.make_async_copy(x_ref.at[:, feat_cols(me)], a_raw.at[rows_of(me), :], own_sem.at[0])
    own_c = pltpu.make_async_copy(cot_ref, call.at[rows_of(me), :], own_sem.at[1])
    own_w = pltpu.make_async_copy(w_ref, buf.at[pl.ds(R, R), :], own_sem.at[2])
    own_x.start()
    own_c.start()
    pl.semaphore_wait(barrier, DP + MP - 2)

    def remote(src, dst, send, recv, **to):
        return pltpu.make_async_remote_copy(
            src_ref=src, dst_ref=dst, send_sem=send, recv_sem=recv,
            device_id=to, device_id_type=MESH,
        )

    def taker(s, d):
        return (s + (MP // 2) * (d % 2)) % MP

    def push(d):
        return remote(x_ref.at[:, feat_cols(d)], a_raw.at[rows_of(me), :],
                      in_send.at[d], in_recv.at[me], dp=d)

    def spread(s, q):
        return remote(a_raw.at[rows_of(s), :], a_raw.at[rows_of(s), :],
                      fwd_send.at[s, q], in_recv.at[s], mp=(m + q) % MP)

    def cot_block(zs, lane, j):
        return call.at[rows_of(zs * 2 + lane), cols_of(j)]

    def up(zs, j, src=None):
        dst = cot_block(zs, c, j)
        return remote(dst if src is None else src, dst, up_send.at[zs, j], lane_recv.at[zs, j], dp=(me + 2) % DP)

    def down(zs, j, src=None):
        dst = cot_block(zs, c, j)
        return remote(dst if src is None else src, dst, dn_send.at[zs, j], lane_recv.at[zs, j], dp=(me + DP - 2) % DP)

    def across(zs, j, src=None):
        dst = cot_block(zs, c, j)
        return remote(dst if src is None else src, dst, sib_send.at[zs, j], sib_recv.at[zs, j], dp=sib)

    def across_in(zs, j):
        dst = cot_block(zs, 1 - c, j)
        return remote(dst, dst, sib_send.at[zs, j], sib_recv.at[zs, j], dp=sib)

    def push_step(d, _):
        @pl.when(jnp.logical_and(d != me, taker(me, d) == m))
        def _():
            push(d).start()
        return 0

    lax.fori_loop(0, DP, push_step, 0)

    DEPTH = 3

    def paced(n):
        k, j = n // NC, n % NC

        @pl.when(n >= 0)
        def _():
            @pl.when(jnp.logical_and(z - k >= 0, z < Z - 1))
            def _():
                up(z - k, j).wait_send()

            @pl.when(jnp.logical_and(z + k < Z, z > 0))
            def _():
                down(z + k, j).wait_send()

    def first_send(j, _):
        src = cot_ref.at[:, cols_of(j)]
        paced(j - DEPTH)

        @pl.when(z < Z - 1)
        def _():
            up(z, j, src).start()

        @pl.when(z > 0)
        def _():
            down(z, j, src).start()

        across(z, j, src).start()
        return 0

    def take_step(s, _):
        @pl.when(jnp.logical_and(s != me, taker(s, me) == m))
        def _():
            spread(s, 1).wait_recv()

            def hand(q, _):
                spread(s, q).start()
                return 0

            lax.fori_loop(1, MP, hand, 0)
        return 0

    early = min(5, NC)
    lax.fori_loop(0, early, first_send, 0)
    own_w.start()
    lax.fori_loop(0, DP, take_step, 0)
    lax.fori_loop(early, NC, first_send, 0)

    def relay(k, j):
        lo, hi = z - k, z + k
        paced(k * NC + j - DEPTH)

        @pl.when(lo >= 0)
        def _():
            up(lo, j).wait_recv()

            @pl.when(z < Z - 1)
            def _():
                up(lo, j).start()

            across(lo, j).start()

        @pl.when(hi < Z)
        def _():
            down(hi, j).wait_recv()

            @pl.when(z > 0)
            def _():
                down(hi, j).start()

            across(hi, j).start()

    def weight_step(j, acc):
        relay(1, j)
        v = buf[R:2 * R, cols_of(j)]
        return acc + jnp.sum((v * v).reshape(R // 8, 8, W), axis=0)

    own_w.wait()
    wacc = lax.fori_loop(0, NC, weight_step, jnp.zeros((8, W), F32))
    s_slots[m, 1] = sum(wacc[:, q * LANES:(q + 1) * LANES] for q in range(G))

    def relay_step(i, _):
        relay(2 + i // NC, i % NC)
        return 0

    lax.fori_loop(0, (Z - 4) * NC, relay_step, 0)

    def rest_step(s, _):
        @pl.when(jnp.logical_and(s != me, taker(s, me) != m))
        def _():
            spread(s, 1).wait_recv()
        return 0

    lax.fori_loop(0, DP, rest_step, 0)
    own_x.wait()
    own_c.wait()

    def turn(i, _):
        cols = pl.ds(pl.multiple_of(i * LANES, LANES), LANES)
        a_t[cols, :] = a_raw[:, cols].T
        return 0

    lax.fori_loop(0, R // LANES, turn, 0)
    row_acc[...] = jnp.zeros_like(row_acc)
    s_acc[...] = jnp.zeros_like(s_acc)

    def col_rows(j):
        return pl.ds(pl.multiple_of(j * G, G), G)

    def col_copy(q, j, own):
        return remote(col_slots.at[own, j], col_slots.at[own, j],
                      col_send.at[q, j], col_recv.at[own, j], dp=(me + q) % DP)

    def s_part(j):
        def got(q, _):
            col_copy(q, j, (me + q) % DP).wait_recv()
            return 0

        lax.fori_loop(1, DP, got, 0)
        tot = lax.fori_loop(1, DP, lambda i, a: a + col_slots[i, j], col_slots[0, j])
        mean = (tot + D * tiny_eps) / D
        inv = []
        for q in range(G):
            row = pl.ds(j * G + q, 1)
            new_cols = decay_rate * cm_ref[row, :] + (1.0 - decay_rate) * mean[q:q + 1, :]
            n_cols[row, :] = new_cols
            inv.append(1.0 / new_cols)

        def s_tile(i, _):
            rows = pl.ds(pl.multiple_of(i * LANES, LANES), LANES)
            part = s_acc[rows, :]
            for q in range(G):
                v = buf[rows, pl.ds(pl.multiple_of(j * W + q * LANES, LANES), LANES)]
                part = part + (v * v) * inv[q]
            s_acc[rows, :] = part
            return 0

        lax.fori_loop(0, RT, s_tile, 0)

    far_z = jnp.where(z >= Z // 2, 0, Z - 1)
    late = T * DP - EARLY
    early_rows = pl.ds(pl.multiple_of(jnp.where(z >= Z // 2, late, 0), late), EARLY)
    late_rows = pl.ds(pl.multiple_of(jnp.where(z >= Z // 2, 0, EARLY), EARLY), late)

    def first_part(j):
        def sib_wait(zs, _):
            @pl.when(zs != far_z)
            def _():
                across_in(zs, j).wait_recv()
            return 0

        lax.fori_loop(0, Z, sib_wait, 0)

        def tile(i, _):
            rows = pl.ds(pl.multiple_of(i * BM, BM), BM)
            buf[rows, cols_of(j)] = jnp.dot(
                a_t[rows, early_rows], call[early_rows, cols_of(j)], preferred_element_type=F32
            )
            return 0

        lax.fori_loop(0, R // BM, tile, 0)

    def chunk(j):
        across_in(far_z, j).wait_recv()

        def tile(i, cacc):
            rows = pl.ds(pl.multiple_of(i * BM, BM), BM)
            gt = buf[rows, cols_of(j)] + jnp.dot(
                a_t[rows, late_rows], call[late_rows, cols_of(j)], preferred_element_type=F32
            )
            buf[rows, cols_of(j)] = gt
            sq = gt * gt
            row_acc[rows, :] += sum(sq[:, q * LANES:(q + 1) * LANES] for q in range(G))
            return cacc + jnp.sum(sq.reshape(BM // 8, 8, W), axis=0)

        cacc = lax.fori_loop(0, R // BM, tile, jnp.zeros((8, W), F32))
        csum = jnp.sum(cacc, axis=0, keepdims=True)
        for q in range(G):
            col_slots[me, j, q:q + 1, :] = csum[:, q * LANES:(q + 1) * LANES]

        def go(q, _):
            col_copy(q, j, me).start()
            return 0

        lax.fori_loop(1, DP, go, 0)

        @pl.when(j >= LAG)
        def _():
            s_part(j - LAG)

    def first_step(j, _):
        relay(Z - 2, j)
        first_part(j)
        return 0

    def last_step(j, _):
        relay(Z - 1, j)
        chunk(j)
        return 0

    lax.fori_loop(0, NC, first_step, 0)
    lax.fori_loop(0, NC, last_step, 0)

    for i in range(RT):
        block = row_acc[i * LANES:(i + 1) * LANES, :].T
        row_slots[m, i:i + 1, :] = jnp.sum(block, axis=0, keepdims=True)

    def share(slots, send, recv, axis, own, count):
        def go(q, _):
            remote(slots.at[own], slots.at[own], send.at[q], recv.at[own], **{axis: (own + q) % count}).start()
            return 0

        lax.fori_loop(1, count, go, 0)

    def shared(slots, send, recv, axis, own, count):
        def done(q, _):
            src = (own + q) % count
            remote(slots.at[src], slots.at[src], send.at[q], recv.at[src], **{axis: src}).wait_recv()
            return 0

        lax.fori_loop(1, count, done, 0)

    def sent(slots, send, recv, axis, own, count):
        def done(q, _):
            remote(slots.at[own], slots.at[own], send.at[q], recv.at[own], **{axis: (own + q) % count}).wait_send()
            return 0

        lax.fori_loop(1, count, done, 0)

    rows_x = (row_slots, row_send, row_recv, "mp", m, MP)
    s_x = (s_slots, s_send, s_recv, "mp", m, MP)
    t_x = (t_slots, t_send, t_recv, "dp", me, DP)

    def total(slots, count):
        return lax.fori_loop(1, count, lambda i, a: a + slots[i], slots[0])

    share(*rows_x)

    def s_rest(j, _):
        s_part(j)
        return 0

    shared(*rows_x)
    new_rows = decay_rate * rm_ref[...] + (1.0 - decay_rate) * ((total(row_slots, MP) + F * tiny_eps) / F)
    buf[at_rows:at_rows + RT, 0:LANES] = new_rows
    inv_rows = 1.0 / new_rows
    for i in range(RT):
        inv_r[i * LANES:(i + 1) * LANES, :] = jnp.broadcast_to(inv_rows[i:i + 1, :], (LANES, LANES)).T
    lax.fori_loop(NC - LAG, NC, s_rest, 0)
    buf[at_cols:at_cols + CT, 0:LANES] = n_cols[...]

    s_slots[m, 0] = jnp.sum((s_acc[...] * inv_r[...]).reshape(R // 8, 8, LANES), axis=0)
    share(*s_x)
    t_slots[me, 2] = jnp.broadcast_to(jnp.sum(new_rows, axis=0, keepdims=True), (8, LANES))
    shared(*s_x)
    t_slots[me, 0:2] = total(s_slots, MP)
    share(*t_x)

    sent(*rows_x)
    sent(*s_x)

    def push_done(d, _):
        @pl.when(jnp.logical_and(d != me, taker(me, d) == m))
        def _():
            push(d).wait_send()

        @pl.when(jnp.logical_and(d != me, taker(d, me) == m))
        def _():
            def hand(q, _):
                spread(d, q).wait_send()
                return 0

            lax.fori_loop(1, MP, hand, 0)
        return 0

    lax.fori_loop(0, DP, push_done, 0)

    def cot_done(i, _):
        across(i // NC, i % NC).wait_send()
        return 0

    lax.fori_loop(0, Z * NC, cot_done, 0)

    def tail_done(i, _):
        paced(Z * NC - DEPTH + i)
        return 0

    lax.fori_loop(0, DEPTH, tail_done, 0)

    def col_done(i, _):
        col_copy(1 + i // NC, i % NC, me).wait_send()
        return 0

    lax.fori_loop(0, (DP - 1) * NC, col_done, 0)

    shared(*t_x)
    sums = total(t_slots, DP)

    def whole(v):
        return jnp.sum(jnp.sum(v, axis=0, keepdims=True), axis=1, keepdims=True)

    row_mean = whole(sums[2, 0:1, :]) / D
    update_rms = jnp.sqrt(row_mean * whole(sums[0]) / (D * F))
    weight_rms = jnp.sqrt(whole(sums[1]) / (D * F))
    factor = jnp.sqrt(row_mean) / jnp.maximum(1.0, update_rms)
    buf[at_scale:at_scale + 8, 0:LANES] = jnp.broadcast_to(factor, (8, LANES))
    buf[at_scale + 8:at_scale + 16, 0:LANES] = jnp.broadcast_to(step_size * weight_rms, (8, LANES))
    sent(*t_x)


def extras(R, C):
    RT, CT = R // LANES, C // LANES
    at_rows = 2 * R
    at_cols = at_rows + -(-RT // 8) * 8
    return at_rows, at_cols, at_cols + -(-CT // 8) * 8


def apply_kernel(R, C, BR, SLOTS, buf, nw_ref, up_ref, nr_ref, nc_ref, rs, cs, nw_buf, up_buf, nw_sem, up_sem):
    RT, CT = R // LANES, C // LANES
    at_rows, at_cols, at_scale = extras(R, C)
    f1 = buf[at_scale:at_scale + 1, 0:LANES]
    f2 = buf[at_scale + 8:at_scale + 9, 0:LANES]
    new_rows = buf[at_rows:at_rows + RT, 0:LANES]
    new_cols = buf[at_cols:at_cols + CT, 0:LANES]
    nr_ref[...] = new_rows
    nc_ref[...] = new_cols
    cs[...] = lax.rsqrt(new_cols)
    inv = lax.rsqrt(new_rows) * f1
    for i in range(RT):
        rs[i * LANES:(i + 1) * LANES, :] = jnp.broadcast_to(inv[i:i + 1, :], (LANES, LANES)).T
    N = R // BR

    def out_copies(i, slot):
        rows = pl.ds(pl.multiple_of(i * BR, BR), BR)
        return (
            pltpu.make_async_copy(nw_buf.at[slot], nw_ref.at[rows, :], nw_sem.at[slot]),
            pltpu.make_async_copy(up_buf.at[slot], up_ref.at[rows, :], up_sem.at[slot]),
        )

    def step(i, _):
        slot = lax.rem(i, SLOTS)

        @pl.when(i >= SLOTS)
        def _():
            for copy in out_copies(i - SLOTS, slot):
                copy.wait()

        g_rows = pl.ds(pl.multiple_of(i * BR, BR), BR)
        w_rows = pl.ds(pl.multiple_of(R + i * BR, BR), BR)
        scale = rs[g_rows, :]
        for q in range(CT):
            sl = slice(q * LANES, (q + 1) * LANES)
            clipped = buf[g_rows, sl] * (scale * cs[q:q + 1, :])
            nw_buf[slot, :, sl] = buf[w_rows, sl] - f2 * clipped
            up_buf[slot, :, sl] = clipped.astype(up_buf.dtype)
        for copy in out_copies(i, slot):
            copy.start()
        return 0

    lax.fori_loop(0, N, step, 0)

    def drain(i, _):
        for copy in out_copies(i, lax.rem(i, SLOTS)):
            copy.wait()
        return 0

    lax.fori_loop(N - SLOTS, N, drain, 0)


def on_device(MP, DP, inputs, cotangent, weight, row_moment, col_moment):
    T = inputs.shape[0]
    R, C = weight.shape
    Z = DP // 2
    W = min(512, C)
    NC = C // W
    G = W // LANES
    BM = min(512, R)
    RT, CT = R // LANES, C // LANES
    height = extras(R, C)[2] + 16
    near = T * (DP - 2)
    early = near // 256 * 256 or near
    vmem = pl.BlockSpec(memory_space=pltpu.VMEM)
    hbm = pl.BlockSpec(memory_space=pl.ANY)
    dma = pltpu.SemaphoreType.DMA
    buf = pl.pallas_call(
        functools.partial(gather_kernel, MP, DP, W, BM, min(4, NC), early),
        out_shape=pltpu.VMEM((height, C), F32),
        in_specs=[hbm, hbm, hbm, vmem, vmem],
        out_specs=vmem,
        scratch_shapes=[
            pltpu.VMEM((T * DP, R), jnp.bfloat16),
            pltpu.VMEM((R, T * DP), jnp.bfloat16),
            pltpu.VMEM((T * DP, C), jnp.bfloat16),
            pltpu.VMEM((R, LANES), F32),
            pltpu.VMEM((R, LANES), F32),
            pltpu.VMEM((R, LANES), F32),
            pltpu.VMEM((CT, LANES), F32),
            pltpu.VMEM((MP, RT, LANES), F32),
            pltpu.VMEM((DP, NC, G, LANES), F32),
            pltpu.VMEM((MP, 2, 8, LANES), F32),
            pltpu.VMEM((DP, 3, 8, LANES), F32),
            dma((3,)), dma((DP,)), dma((DP,)), dma((DP, MP)),
            dma((Z, NC)), dma((Z, NC)), dma((Z, NC)), dma((Z, NC)), dma((Z, NC)),
            dma((MP,)), dma((MP,)), dma((DP, NC)), dma((DP, NC)),
            dma((MP,)), dma((MP,)), dma((DP,)), dma((DP,)),
        ],
        compiler_params=pltpu.CompilerParams(
            collective_id=0, has_side_effects=True, vmem_limit_bytes=28 * 2**20
        ),
        cost_estimate=pl.CostEstimate(flops=2 * R * C * T * DP, bytes_accessed=R * C * 4, transcendentals=0),
        name="gather_contract",
    )(inputs, cotangent, weight, row_moment.reshape(RT, LANES), col_moment.reshape(CT, LANES))
    BR = min(64, R)
    SLOTS = min(3, R // BR)
    new_weight, update, nr, nc = pl.pallas_call(
        functools.partial(apply_kernel, R, C, BR, SLOTS),
        out_shape=[
            jax.ShapeDtypeStruct((R, C), F32),
            jax.ShapeDtypeStruct((R, C), jnp.bfloat16),
            jax.ShapeDtypeStruct((RT, LANES), F32),
            jax.ShapeDtypeStruct((CT, LANES), F32),
        ],
        in_specs=[vmem],
        out_specs=[hbm, hbm, vmem, vmem],
        scratch_shapes=[
            pltpu.VMEM((R, LANES), F32),
            pltpu.VMEM((CT, LANES), F32),
            pltpu.VMEM((SLOTS, BR, C), F32),
            pltpu.VMEM((SLOTS, BR, C), jnp.bfloat16),
            dma((SLOTS,)), dma((SLOTS,)),
        ],
        compiler_params=pltpu.CompilerParams(vmem_limit_bytes=16 * 2**20),
        cost_estimate=pl.CostEstimate(flops=4 * R * C, bytes_accessed=R * C * 6, transcendentals=0),
        name="apply_update",
    )(buf)
    return new_weight, update, nr.reshape(R), nc.reshape(C)


def solution(mesh):
    return jax.shard_map(
        functools.partial(on_device, mesh.shape["mp"], mesh.shape["dp"]),
        mesh=mesh,
        in_specs=(P("dp", None), P("dp", "mp"), P("dp", "mp"), P("dp"), P("mp")),
        out_specs=(P("dp", "mp"), P("dp", "mp"), P("dp"), P("mp")),
        check_vma=False,
    )
```
